32 devices in a mesh: row: 4 (over y, x), col: 8 (over z, core).
Axes of the slice: x: 2, y: 2, z: 4, core: 2. Of those that a mesh axis runs over, the one named last changes fastest.
Arguments:
- queries: bfloat16 [4096, 2048], P(('row', 'col')), may hold values from -6 to 6
- keys: bfloat16 [4096, 2048], P(('row', 'col')), may hold values from -6 to 6
- values: bfloat16 [4096, 2048], P(('row', 'col')), may hold values from -6 to 6
- grad_out: bfloat16 [4096, 2048], P(('row', 'col')), may hold values from -6 to 6
- conv_weight: float32 [4, 2048], replicated, may hold values from -3 to 3
Outputs:
- grad_queries: bfloat16 [4096, 2048], P(('row', 'col'))
- grad_keys: bfloat16 [4096, 2048], P(('row', 'col'))
- grad_values: bfloat16 [4096, 2048], P(('row', 'col'))
- grad_weight: float32 [4, 2048], replicated
The draws below stay inside these ranges and needn't reach their ends.
All inputs are finite; a program needn't handle non-finite values.
Results may differ from the reference program's by a relative error of at most 0.025.
Values may be sent and summed in bfloat16 or wider, within the bound.
No kernel may reach another device: no remote copies, remote signals or barrier semaphores. Data moves between devices by JAX's collectives and lax.ppermute only.
A program may use at most 192 MiB of HBM per device.

```python
import jax
import jax.numpy as jnp
from jax import lax

HEADS = 16
DH = 128
CW = 4
TOK_DEV = 128
D = 2048
TOKENS = 4096


def steps_of(own_key, shape, cuts, smallest, high):
    level, own = 1.0, jax.random.fold_in(own_key, 6)
    for dim, blocks in cuts:
        heights = jnp.exp(jax.random.uniform(jax.random.fold_in(own, dim), (blocks,), jnp.float32, smallest / len(cuts), high / len(cuts)))
        level = level * jnp.repeat(heights, shape[dim] // blocks).reshape([-1 if axis == dim else 1 for axis in range(len(shape))])
    return level


def gaussian(key, dims, width, limit, pieces=(), dtype=jnp.bfloat16):
    entries = width * jax.random.normal(key, dims, jnp.float32)
    if pieces:
        entries = entries * steps_of(key, dims, pieces, -0.22, 0.18)
    return jnp.clip(entries, -limit, limit).astype(dtype)


def setup_inputs(seed: int = 0) -> dict:
    arg_keys = jax.random.split(jax.random.key(seed), 6)
    return {
        "queries": gaussian(arg_keys[0], (TOKENS, D), 1.0, 6.0, ((0, 32),)),
        "keys": gaussian(arg_keys[1], (TOKENS, D), 1.0, 6.0, ((0, 32),)),
        "values": gaussian(arg_keys[2], (TOKENS, D), 1.0, 6.0, ((0, 32),)),
        "grad_out": gaussian(arg_keys[3], (TOKENS, D), 1.0, 6.0, ((0, 32),)),
        "conv_weight": gaussian(arg_keys[4], (CW, D), 0.5, 3.0, (), jnp.float32),
    }


def reference(queries, keys, values, grad_out, conv_weight):
    total = queries.shape[0]
    rows = TOK_DEV
    blocks = total // rows
    scale = (DH * total) ** -0.5
    value_pad = jnp.pad(values.astype(jnp.float32), ((CW - 1, 0), (0, 0)))
    conv_acc = jnp.zeros((total, HEADS * DH), jnp.float32)
    for offset in range(CW):
        conv_acc = conv_acc + conv_weight[offset][None, :] * value_pad[CW - 1 - offset:CW - 1 - offset + total]
    conved = conv_acc.astype(jnp.bfloat16)
    query_blocks = queries.reshape(blocks, rows, HEADS, DH)
    key_blocks = keys.reshape(blocks, rows, HEADS, DH)
    conv_blocks = conved.reshape(blocks, rows, HEADS, DH)
    grad_blocks = grad_out.reshape(blocks, rows, HEADS, DH)

    def local_states(items):
        query_part, key_part, conv_part, grad_part = items
        key_state = jnp.einsum("thd,the->hde", key_part.astype(jnp.float32), conv_part.astype(jnp.float32))
        query_state = jnp.einsum("thd,the->hde", query_part.astype(jnp.float32), grad_part.astype(jnp.float32))
        return key_state, query_state

    key_states, query_states = lax.map(local_states, (query_blocks, key_blocks, conv_blocks, grad_blocks))
    zero_state = jnp.zeros((HEADS, DH, DH), jnp.float32)

    def carry_on(carry, state):
        return carry + state, carry

    _, prefix = lax.scan(carry_on, zero_state, key_states)
    _, suffix = lax.scan(carry_on, zero_state, query_states, reverse=True)
    positions = jnp.arange(rows)
    causal = (positions[:, None] >= positions[None, :])[None, :, :]

    def block_grads(items):
        query_part, key_part, conv_part, grad_part, prefix_part, suffix_part = items
        query_f = query_part.astype(jnp.float32)
        key_f = key_part.astype(jnp.float32)
        conv_f = conv_part.astype(jnp.float32)
        grad_f = grad_part.astype(jnp.float32)
        attn = jnp.where(causal, jnp.einsum("thd,uhd->htu", grad_f, conv_f), 0.0).astype(jnp.bfloat16).astype(jnp.float32)
        score = jnp.where(causal, jnp.einsum("thd,uhd->htu", query_f, key_f), 0.0).astype(jnp.bfloat16).astype(jnp.float32)
        prefix_f = prefix_part.astype(jnp.bfloat16).astype(jnp.float32)
        suffix_f = suffix_part.astype(jnp.bfloat16).astype(jnp.float32)
        grad_query = scale * (jnp.einsum("htu,uhd->thd", attn, key_f) + jnp.einsum("the,hde->thd", grad_f, prefix_f))
        grad_key = scale * (jnp.einsum("htu,thd->uhd", attn, query_f) + jnp.einsum("the,hde->thd", conv_f, suffix_f))
        grad_conv = scale * (jnp.einsum("htu,thd->uhd", score, grad_f) + jnp.einsum("thd,hde->the", key_f, suffix_f))
        return grad_query.astype(jnp.bfloat16), grad_key.astype(jnp.bfloat16), grad_conv

    grad_query, grad_key, grad_conv = lax.map(block_grads, (query_blocks, key_blocks, conv_blocks, grad_blocks, prefix, suffix))
    grad_query = grad_query.reshape(total, HEADS * DH)
    grad_key = grad_key.reshape(total, HEADS * DH)
    grad_conv = grad_conv.reshape(total, HEADS * DH)
    grad_pad = jnp.pad(grad_conv, ((0, CW - 1), (0, 0)))
    value_acc = jnp.zeros((total, HEADS * DH), jnp.float32)
    weight_rows = []
    for offset in range(CW):
        value_acc = value_acc + conv_weight[offset][None, :] * grad_pad[offset:offset + total]
        weight_rows.append(jnp.sum(grad_conv * value_pad[CW - 1 - offset:CW - 1 - offset + total], axis=0))
    grad_weight = jnp.stack(weight_rows, axis=0)
    return grad_query, grad_key, value_acc.astype(jnp.bfloat16), grad_weight
```

```python
import functools

import jax
import jax.numpy as jnp
from jax import lax
from jax.experimental import pallas as pl
from jax.experimental.pallas import tpu as pltpu
from jax.sharding import PartitionSpec as P

HEADS = 16
DH = 128
CW = 4
HALF = HEADS // 2
HALO = 8
AXES = ("row", "col")
F32 = jnp.float32
BF16 = jnp.bfloat16
VMEM = pl.BlockSpec(memory_space=pltpu.VMEM)
SMEM = pl.BlockSpec(memory_space=pltpu.SMEM)
PARAMS = pltpu.CompilerParams(vmem_limit_bytes=40 * 1024 * 1024)


def dot(a, b, over):
    return lax.dot_general(a, b, ((over[:1], over[1:]), ((), ())), preferred_element_type=F32)


def columns(head):
    return pl.ds(pl.multiple_of(head * DH, DH), DH)


def call(kernel, outs, scalars, arrays, scratch=()):
    return pl.pallas_call(
        kernel,
        out_shape=outs,
        in_specs=[SMEM] * len(scalars) + [VMEM] * len(arrays),
        out_specs=jax.tree.map(lambda _: VMEM, outs),
        scratch_shapes=scratch,
        compiler_params=PARAMS,
    )(*scalars, *arrays)


def shape(dims, dtype=BF16):
    return jax.ShapeDtypeStruct(dims, dtype)


def query_state_kernel(core_ref, q_ref, g_ref, keep_ref, send_ref):
    core = core_ref[0]
    for side, out in enumerate((keep_ref, send_ref)):
        first = HALF * lax.rem(core + side, 2)
        for i in range(HALF):
            at = columns(first + i)
            out[i] = dot(q_ref[:, at], g_ref[:, at], (0, 0)).astype(BF16)


def key_state_kernel(core_ref, k_ref, v_ref, halo_ref, w_ref, conv_ref, keep_ref, send_ref):
    core = core_ref[0]
    rows = v_ref.shape[0]
    for side, out in enumerate((keep_ref, send_ref)):
        first = HALF * lax.rem(core + side, 2)
        for i in range(HALF):
            at = columns(first + i)
            ext = jnp.concatenate([halo_ref[:, at].astype(F32), v_ref[:, at].astype(F32)], axis=0)
            acc = w_ref[pl.ds(0, 1), at] * ext[HALO:]
            for j in range(1, CW):
                acc = acc + w_ref[pl.ds(j, 1), at] * ext[HALO - j : HALO - j + rows]
            conved = acc.astype(BF16)
            conv_ref[:, at] = conved
            out[i] = dot(k_ref[:, at], conved, (0, 0)).astype(BF16)


def turn_kernel(q_ref, keep_ref, recv_ref, out_ref):
    chips = q_ref.shape[0]
    total = jnp.zeros(q_ref.shape[1:], F32)
    for p in reversed(range(chips)):
        out_ref[p, 0] = total.astype(BF16)
        total = total + q_ref[p].astype(F32)
        out_ref[p, 1] = (keep_ref[p].astype(F32) + recv_ref[p].astype(F32)).astype(BF16)


def share_kernel(core_ref, chip_ref, keep_ref, recv_ref, own_ref, send_ref, *, first_gets):
    core = core_ref[0]
    mine = (core == (0 if first_gets else 1)).astype(F32)
    for p in range(chip_ref.shape[0]):
        state = chip_ref[p, 0].astype(F32)
        own_ref[p] = (state + mine * recv_ref[p].astype(F32)).astype(BF16)
        send_ref[p] = (state + (1.0 - mine) * keep_ref[p].astype(F32)).astype(BF16)


def query_side_kernel(
    core_ref,
    q_ref,
    k_ref,
    c_ref,
    g_ref,
    v_ref,
    halo_ref,
    own_ref,
    recv_ref,
    chip_ref,
    gk_ref,
    gc_ref,
    edge_ref,
    out_ref,
    taps_ref,
    *,
    scale,
):
    core = core_ref[0]
    rows = q_ref.shape[0]
    early = lax.broadcasted_iota(jnp.int32, (rows, rows), 0) <= lax.broadcasted_iota(
        jnp.int32, (rows, rows), 1
    )
    for side, states in enumerate((own_ref, recv_ref)):
        first = HALF * lax.rem(core + side, 2)
        for i in range(HALF):
            head = first + i
            at = columns(head)
            q, k, c, g, suffix = q_ref[:, at], k_ref[:, at], c_ref[:, at], g_ref[:, at], states[i]
            score = jnp.where(early, dot(k, q, (1, 1)), 0.0).astype(BF16)
            attn = jnp.where(early, dot(c, g, (1, 1)), 0.0).astype(BF16)
            gk = dot(attn, q, (1, 0)) + dot(c, suffix, (1, 1))
            gk_ref[:, at] = (scale * gk).astype(BF16)
            gc = scale * (dot(score, g, (1, 0)) + dot(k, suffix, (1, 0)))
            gc_ref[:, at] = gc
            edge_ref[:, at] = gc[:HALO]
            ext = jnp.concatenate([halo_ref[:, at].astype(F32), v_ref[:, at].astype(F32)], axis=0)
            for j in range(CW):
                part = jnp.sum(gc * ext[HALO - j : HALO - j + rows], axis=0, keepdims=True)
                taps_ref[pl.ds(j * HEADS + head, 1), :] = part
    chips, pieces, depth, _ = out_ref.shape
    total = jnp.zeros(out_ref.shape[2:], F32)
    taps = [taps_ref[n * depth : (n + 1) * depth].astype(BF16) for n in range(pieces - 1)]
    for p in range(chips):
        out_ref[p, 0] = total.astype(BF16)
        total = total + chip_ref[p, 1].astype(F32)
        for n in range(pieces - 1):
            out_ref[p, 1 + n] = taps[n]


def taps_kernel(chip_ref, out_ref):
    chips, pieces, depth, _ = chip_ref.shape
    for n in range(pieces - 1):
        total = chip_ref[0, 1 + n].astype(F32)
        for p in range(1, chips):
            total = total + chip_ref[p, 1 + n].astype(F32)
        out_ref[n * depth : (n + 1) * depth] = total


def key_side_kernel(
    core_ref,
    k_ref,
    c_ref,
    g_ref,
    own_ref,
    recv_ref,
    gc_ref,
    edge_ref,
    w_ref,
    taps_ref,
    far_ref,
    gq_ref,
    gv_ref,
    gw_ref,
    *,
    scale,
):
    core = core_ref[0]
    rows = k_ref.shape[0]
    causal = lax.broadcasted_iota(jnp.int32, (rows, rows), 0) >= lax.broadcasted_iota(
        jnp.int32, (rows, rows), 1
    )
    for side, states in enumerate((own_ref, recv_ref)):
        first = HALF * lax.rem(core + side, 2)
        for i in range(HALF):
            at = columns(first + i)
            k, c, g, prefix = k_ref[:, at], c_ref[:, at], g_ref[:, at], states[i]
            attn = jnp.where(causal, dot(g, c, (1, 1)), 0.0).astype(BF16)
            gq = dot(attn, k, (1, 0)) + dot(g, prefix, (1, 1))
            gq_ref[:, at] = (scale * gq).astype(BF16)
            ext = jnp.concatenate([gc_ref[:, at], edge_ref[:, at]], axis=0)
            acc = w_ref[pl.ds(0, 1), at] * ext[:rows]
            for j in range(1, CW):
                acc = acc + w_ref[pl.ds(j, 1), at] * ext[j : j + rows]
            gv_ref[:, at] = acc.astype(BF16)
    for head in range(HEADS):
        for j in range(CW):
            row = pl.ds(j * HEADS + head, 1)
            gw_ref[pl.ds(j, 1), pl.ds(head * DH, DH)] = taps_ref[row, :] + far_ref[row, :]


def local(queries, keys, values, grad_out, conv_weight):
    rows, width = queries.shape
    count = lax.axis_size("row") * lax.axis_size("col")
    chips = count // 2
    depth = HALF * DH // chips
    pieces = 1 + CW * HEADS // depth
    scale = (DH * rows * count) ** (-0.5)
    core = lax.rem(lax.axis_index("col"), 2).astype(jnp.int32).reshape(1)
    groups = [[2 * p + c for p in range(chips)] for c in range(2)]

    def swap(value):
        return lax.ppermute(value, AXES, [(d, d ^ 1) for d in range(count)])

    def shifted(value, by):
        pairs = [(d, d + by) for d in range(count) if 0 <= d + by < count]
        return lax.ppermute(value, AXES, pairs)

    def turn(value):
        return lax.all_to_all(value, AXES, 0, 0, axis_index_groups=groups, tiled=True)

    def sliced(value):
        return value.reshape(chips, depth, DH)

    def headed(value):
        return value.reshape(HALF, DH, DH)

    half = shape((HALF, DH, DH))
    slices = shape((chips, depth, DH))
    halo = shifted(values[rows - HALO :], 1)
    q_keep, q_send = call(query_state_kernel, (half, half), [core], [queries, grad_out])
    q_recv = swap(q_send)
    conved, k_keep, k_send = call(
        key_state_kernel,
        (shape((rows, width)), half, half),
        [core],
        [keys, values, halo, conv_weight],
    )
    k_recv = swap(k_send)
    q_chip = (q_keep.astype(F32) + q_recv.astype(F32)).astype(BF16)
    q_turned = turn(sliced(q_chip))
    both = call(
        turn_kernel,
        shape((chips, 2, depth, DH)),
        [],
        [q_turned, sliced(k_keep), sliced(k_recv)],
    )
    both = turn(both)
    q_own, q_give = call(
        functools.partial(share_kernel, first_gets=True),
        (slices, slices),
        [core],
        [both, sliced(q_keep), sliced(q_recv)],
    )
    q_got = swap(q_give)
    grad_keys, grad_conv, edge, last = call(
        functools.partial(query_side_kernel, scale=scale),
        (
            shape((rows, width)),
            shape((rows, width), F32),
            shape((HALO, width), F32),
            shape((chips, pieces, depth, DH)),
        ),
        [core],
        [
            queries,
            keys,
            conved,
            grad_out,
            values,
            halo,
            headed(q_own),
            headed(q_got),
            both,
        ],
        [pltpu.VMEM((CW * HEADS, DH), F32)],
    )
    edge = shifted(edge, -1)
    last = turn(last)
    k_own, k_give = call(
        functools.partial(share_kernel, first_gets=False),
        (slices, slices),
        [core],
        [last, sliced(k_keep), sliced(k_recv)],
    )
    k_got = swap(k_give)
    taps = call(taps_kernel, shape((CW * HEADS, DH), F32), [], [last])
    far = swap(taps)
    grad_queries, grad_values, grad_weight = call(
        functools.partial(key_side_kernel, scale=scale),
        (shape((rows, width)), shape((rows, width)), shape((CW, width), F32)),
        [core],
        [
            keys,
            conved,
            grad_out,
            headed(k_own),
            headed(k_got),
            grad_conv,
            edge,
            conv_weight,
            taps,
            far,
        ],
    )
    return grad_queries, grad_keys, grad_values, grad_weight


def solution(mesh):
    placed = (
        P(("row", "col"), None),
        P(("row", "col"), None),
        P(("row", "col"), None),
        P(("row", "col"), None),
        P(),
    )
    return jax.shard_map(
        local,
        mesh=mesh,
        in_specs=placed,
        out_specs=(P(("row", "col"), None), P(("row", "col"), None), P(("row", "col"), None), P()),
        check_vma=False,
    )
```

```python
import functools

import jax
import jax.numpy as jnp
from jax import lax
from jax.experimental import pallas as pl
from jax.experimental.pallas import tpu as pltpu
from jax.sharding import PartitionSpec as P

HEADS = 16
DH = 128
CW = 4
HALF = HEADS // 2
WIDE = HALF * DH
EDGE = 8
HALO = 16
AXES = ("row", "col")
F32 = jnp.float32
BF16 = jnp.bfloat16
VMEM = pl.BlockSpec(memory_space=pltpu.VMEM)
SMEM = pl.BlockSpec(memory_space=pltpu.SMEM)
ANY = pl.BlockSpec(memory_space=pl.ANY)
PARAMS = pltpu.CompilerParams(vmem_limit_bytes=48 * 1024 * 1024)


def dot(a, b, over):
    return lax.dot_general(a, b, ((over[:1], over[1:]), ((), ())), preferred_element_type=F32)


def columns(head):
    return pl.ds(head * DH, DH)


def half_of(core, size):
    return pl.ds(pl.multiple_of(core * size, size), size)


def call(kernel, outs, core, arrays, scratch=(), space=VMEM):
    return pl.pallas_call(
        kernel,
        out_shape=outs,
        in_specs=[SMEM] + [space] * len(arrays),
        out_specs=jax.tree.map(lambda _: VMEM, outs),
        scratch_shapes=scratch,
        compiler_params=PARAMS,
    )(core, *arrays)


def shape(dims, dtype=BF16):
    return jax.ShapeDtypeStruct(dims, dtype)


def split_kernel(core_ref, a_ref, b_ref, own_ref, send_ref, sems):
    core = core_ref[0]
    copies = []
    for n, ref in enumerate((a_ref, b_ref)):
        for m, (out, side) in enumerate(((send_ref, 1 - core), (own_ref, core))):
            copies.append(
                pltpu.make_async_copy(ref.at[:, half_of(side, WIDE)], out.at[n], sems.at[n, m])
            )
    for copy in copies:
        copy.start()
    for copy in copies:
        copy.wait()


def query_state_kernel(core_ref, own_ref, recv_ref, q_ref, g_ref, state_ref):
    core = core_ref[0]
    rows = own_ref.shape[1]
    for n, ref in enumerate((q_ref, g_ref)):
        ref[half_of(core, rows), :] = own_ref[n]
        ref[half_of(1 - core, rows), :] = recv_ref[n]
    for i in range(HALF):
        at = columns(i)
        state_ref[i] = dot(q_ref[:, at], g_ref[:, at], (0, 0)).astype(BF16)


def gather_kernel(core_ref, own_ref, recv_ref, k_ref, v_ref, tail_ref):
    core = core_ref[0]
    rows = own_ref.shape[1]
    for n, ref in enumerate((k_ref, v_ref)):
        ref[half_of(core, rows), :] = own_ref[n]
        ref[half_of(1 - core, rows), :] = recv_ref[n]
    tail_ref[...] = v_ref[2 * rows - HALO :, :]


def lagged(v_ref, halo_ref, at):
    ext = jnp.concatenate([halo_ref[:, at].astype(F32), v_ref[:, at].astype(F32)], axis=0)
    rows = v_ref.shape[0]
    return [ext[HALO - j : HALO - j + rows] for j in range(CW)]


def inner_kernel(
    core_ref,
    q_ref,
    g_ref,
    k_ref,
    v_ref,
    halo_ref,
    w_ref,
    qs_ref,
    c_ref,
    state_ref,
    gq_ref,
    gk_ref,
    gc_ref,
    edge_ref,
):
    core = core_ref[0]
    rows = q_ref.shape[0]
    first = lax.broadcasted_iota(jnp.int32, (rows, rows), 0)
    second = lax.broadcasted_iota(jnp.int32, (rows, rows), 1)
    for i in range(HALF):
        at = columns(i)
        taps = w_ref[:, pl.ds(pl.multiple_of(core * WIDE + i * DH, DH), DH)]
        parts = lagged(v_ref, halo_ref, at)
        acc = taps[0:1] * parts[0]
        for j in range(1, CW):
            acc = acc + taps[j : j + 1] * parts[j]
        c = acc.astype(BF16)
        c_ref[:, at] = c
        q, g, k = q_ref[:, at], g_ref[:, at], k_ref[:, at]
        state_ref[i] = dot(k, c, (0, 0)).astype(BF16)
        score = jnp.where(first <= second, dot(k, q, (1, 1)), 0.0).astype(BF16)
        turned = jnp.where(first <= second, dot(c, g, (1, 1)), 0.0).astype(BF16)
        attn = jnp.where(first >= second, dot(g, c, (1, 1)), 0.0).astype(BF16)
        gq_ref[:, at] = dot(attn, k, (1, 0))
        gk_ref[:, at] = dot(turned, q, (1, 0))
        gc = dot(score, g, (1, 0))
        gc_ref[:, at] = gc
        edge_ref[:EDGE, at] = (gc[:HALO] - dot(k[:HALO], qs_ref[i], (1, 0)))[:EDGE]
        edge_ref[EDGE:, at] = k[:HALO].astype(F32)[:EDGE]


def turn_kernel(core_ref, q_ref, state_ref, out_ref):
    total = jnp.zeros(q_ref.shape[1:], F32)
    for p in reversed(range(q_ref.shape[0])):
        out_ref[p, 0] = total.astype(BF16)
        total = total + q_ref[p].astype(F32)
        out_ref[p, 1] = state_ref[p]


def head_state(read, head, depth):
    parts = DH // depth
    if depth % HALO == 0:
        return jnp.concatenate([read(head * parts + n) for n in range(parts)], axis=0)
    found = [read(head * parts + n).astype(F32) for n in range(parts)]
    return jnp.concatenate(found, axis=0).astype(BF16)


def query_side_kernel(
    core_ref,
    chip_ref,
    k_ref,
    c_ref,
    v_ref,
    halo_ref,
    gk_ref,
    gc_ref,
    edge_ref,
    w_ref,
    own_ref,
    send_ref,
    out_ref,
    taps_ref,
    *,
    scale,
):
    core = core_ref[0]
    rows = k_ref.shape[0]
    chips, _, depth, _ = chip_ref.shape
    for i in range(HALF):
        at = columns(i)
        suffix = head_state(lambda p: chip_ref[p, 0], i, depth)
        gk = scale * (gk_ref[:, at] + dot(c_ref[:, at], suffix, (1, 1)))
        gc = scale * (gc_ref[:, at] + dot(k_ref[:, at], suffix, (1, 0)))
        after = dot(edge_ref[EDGE:, at].astype(BF16), suffix, (1, 0))
        ext = jnp.concatenate([gc, scale * (edge_ref[:EDGE, at] + after)], axis=0)
        taps = w_ref[:, pl.ds(pl.multiple_of(core * WIDE + i * DH, DH), DH)]
        gv = taps[0:1] * gc
        for j in range(1, CW):
            gv = gv + taps[j : j + 1] * ext[j : j + rows]
        for n, value in enumerate((gk, gv)):
            low, high = value[: rows // 2].astype(BF16), value[rows // 2 :].astype(BF16)
            own_ref[n, :, at] = jnp.where(core == 0, low, high)
            send_ref[n, :, at] = jnp.where(core == 0, high, low)
        for j, part in enumerate(lagged(v_ref, halo_ref, at)):
            taps_ref[j * HALF + i : j * HALF + i + 1, :] = jnp.sum(gc * part, axis=0, keepdims=True)
    total = jnp.zeros((depth, DH), F32)
    weights = taps_ref[...].astype(BF16)
    start = out_ref.shape[1] - CW * HALF
    for p in range(chips):
        out_ref[p, :depth] = total.astype(BF16)
        total = total + chip_ref[p, 1].astype(F32)
        out_ref[p, start:] = weights


def key_side_kernel(
    core_ref, chip_ref, g_ref, gq_ref, own_ref, send_ref, taps_ref, *, scale, depth
):
    core = core_ref[0]
    rows = g_ref.shape[0]
    chips, size, _ = chip_ref.shape
    for i in range(HALF):
        at = columns(i)
        prefix = head_state(lambda p: chip_ref[p, :depth], i, depth)
        gq = scale * (gq_ref[:, at] + dot(g_ref[:, at], prefix, (1, 1)))
        low, high = gq[: rows // 2].astype(BF16), gq[rows // 2 :].astype(BF16)
        own_ref[:, at] = jnp.where(core == 0, low, high)
        send_ref[:, at] = jnp.where(core == 0, high, low)
    total = chip_ref[0, size - CW * HALF :].astype(F32)
    for p in range(1, chips):
        total = total + chip_ref[p, size - CW * HALF :].astype(F32)
    taps_ref[...] = total


def join_kernel(core_ref, own_ref, recv_ref, a_ref, b_ref):
    core = core_ref[0]
    for n, ref in enumerate((a_ref, b_ref)):
        ref[:, half_of(core, WIDE)] = own_ref[n]
        ref[:, half_of(1 - core, WIDE)] = recv_ref[n]


def finish_kernel(core_ref, own_ref, recv_ref, taps_ref, far_ref, gq_ref, gw_ref):
    core = core_ref[0]
    gq_ref[:, half_of(core, WIDE)] = own_ref[...]
    gq_ref[:, half_of(1 - core, WIDE)] = recv_ref[...]
    for side, ref in ((core, taps_ref), (1 - core, far_ref)):
        for i in range(HALF):
            at = pl.ds(pl.multiple_of(side * WIDE + i * DH, DH), DH)
            for j in range(CW):
                row = j * HALF + i
                gw_ref[j : j + 1, at] = ref[row : row + 1, :]


def local(queries, keys, values, grad_out, conv_weight):
    rows, width = queries.shape
    count = lax.axis_size("row") * lax.axis_size("col")
    chips = count // 2
    depth = WIDE // chips
    scale = (DH * rows * count) ** (-0.5)
    core = lax.rem(lax.axis_index("col"), 2).astype(jnp.int32).reshape(1)
    groups = [[2 * p + c for p in range(chips)] for c in range(2)]

    def swap(value):
        return lax.ppermute(value, AXES, [(d, d ^ 1) for d in range(count)])

    def shifted(value, by):
        pairs = [(d, d + by) for d in range(count) if 0 <= d + by < count]
        return lax.ppermute(value, AXES, pairs)

    def turn(value):
        return lax.all_to_all(value, AXES, 0, 0, axis_index_groups=groups, tiled=True)

    pair = shape((2, rows, WIDE))
    block = shape((2 * rows, WIDE))
    block32 = shape((2 * rows, WIDE), F32)
    states = shape((HALF, DH, DH))
    sems = [pltpu.SemaphoreType.DMA((2, 2))]
    qg_own, qg_send = call(split_kernel, (pair, pair), core, [queries, grad_out], sems, ANY)
    qg_recv = swap(qg_send)
    kv_own, kv_send = call(split_kernel, (pair, pair), core, [keys, values], sems, ANY)
    kv_recv = swap(kv_send)
    q, g, q_state = call(query_state_kernel, (block, block, states), core, [qg_own, qg_recv])
    q_turned = turn(q_state.reshape(chips, depth, DH))
    k, v, tail = call(
        gather_kernel, (block, block, shape((HALO, WIDE))), core, [kv_own, kv_recv]
    )
    halo = shifted(tail, 2)
    c, k_state, gq, gk, gc, edge = call(
        inner_kernel,
        (block, states, block32, block32, block32, shape((2 * EDGE, WIDE), F32)),
        core,
        [q, g, k, v, halo, conv_weight, q_state],
    )
    edge = shifted(edge, -2)
    both = call(
        turn_kernel,
        shape((chips, 2, depth, DH)),
        core,
        [q_turned, k_state.reshape(chips, depth, DH)],
    )
    both = turn(both)
    kv_grad, kv_give, last = call(
        functools.partial(query_side_kernel, scale=scale),
        (pair, pair, shape((chips, max(depth, HALO) + CW * HALF, DH))),
        core,
        [both, k, c, v, halo, gk, gc, edge, conv_weight],
        [pltpu.VMEM((CW * HALF, DH), F32)],
    )
    kv_got = swap(kv_give)
    last = turn(last)
    q_grad, q_give, taps = call(
        functools.partial(key_side_kernel, scale=scale, depth=depth),
        (shape((rows, WIDE)), shape((rows, WIDE)), shape((CW * HALF, DH), F32)),
        core,
        [last, g, gq],
    )
    q_got = swap(q_give)
    far = swap(taps)
    full = shape((rows, width))
    grad_keys, grad_values = call(join_kernel, (full, full), core, [kv_grad, kv_got])
    grad_queries, grad_weight = call(
        finish_kernel, (full, shape((CW, width), F32)), core, [q_grad, q_got, taps, far]
    )
    return grad_queries, grad_keys, grad_values, grad_weight


def solution(mesh):
    placed = (
        P(("row", "col"), None),
        P(("row", "col"), None),
        P(("row", "col"), None),
        P(("row", "col"), None),
        P(),
    )
    return jax.shard_map(
        local,
        mesh=mesh,
        in_specs=placed,
        out_specs=(P(("row", "col"), None), P(("row", "col"), None), P(("row", "col"), None), P()),
        check_vma=False,
    )
```

```python
import functools

import jax
import jax.numpy as jnp
from jax import lax
from jax.experimental import pallas as pl
from jax.experimental.pallas import tpu as pltpu
from jax.sharding import PartitionSpec as P

HEADS = 16
DH = 128
CW = 4
HALF = HEADS // 2
WIDE = HALF * DH
EDGE = 8
HALO = 16
AXES = ("row", "col")
F32 = jnp.float32
BF16 = jnp.bfloat16
VMEM = pl.BlockSpec(memory_space=pltpu.VMEM)
SMEM = pl.BlockSpec(memory_space=pltpu.SMEM)
HBM = pl.BlockSpec(memory_space=pl.ANY)
PARAMS = pltpu.CompilerParams(vmem_limit_bytes=16 * 1024 * 1024)


def dot(a, b, over):
    return lax.dot_general(a, b, ((over[:1], over[1:]), ((), ())), preferred_element_type=F32)


def columns(head):
    return pl.ds(head * DH, DH)


def half_of(core, size):
    return pl.ds(pl.multiple_of(core * size, size), size)


def call(kernel, outs, core, arrays, scratch=(), space=VMEM):
    return pl.pallas_call(
        kernel,
        out_shape=outs,
        in_specs=[SMEM] + [space] * len(arrays),
        out_specs=jax.tree.map(lambda _: VMEM, outs),
        scratch_shapes=scratch,
        compiler_params=PARAMS,
    )(core, *arrays)


def shape(dims, dtype=BF16):
    return jax.ShapeDtypeStruct(dims, dtype)


def split_kernel(core_ref, a_ref, b_ref, own_ref, send_ref, sems):
    core = core_ref[0]
    copies = []
    for n, ref in enumerate((a_ref, b_ref)):
        for m, (out, side) in enumerate(((send_ref, 1 - core), (own_ref, core))):
            copies.append(
                pltpu.make_async_copy(ref.at[:, half_of(side, WIDE)], out.at[n], sems.at[n, m])
            )
    for copy in copies:
        copy.start()
    for copy in copies:
        copy.wait()


def gather(core, own_ref, recv_ref, refs):
    rows = own_ref.shape[1]
    for n, ref in enumerate(refs):
        ref[half_of(core, rows), :] = own_ref[n]
        ref[half_of(1 - core, rows), :] = recv_ref[n]


def query_state_kernel(core_ref, own_ref, recv_ref, q_ref, g_ref, state_ref):
    gather(core_ref[0], own_ref, recv_ref, (q_ref, g_ref))
    for i in range(HALF):
        at = columns(i)
        state_ref[i] = dot(q_ref[:, at], g_ref[:, at], (0, 0)).astype(BF16)


def gather_kernel(core_ref, own_ref, recv_ref, k_ref, v_ref, tail_ref):
    gather(core_ref[0], own_ref, recv_ref, (k_ref, v_ref))
    tail_ref[...] = v_ref[v_ref.shape[0] - HALO :, :]


def lagged(v_ref, halo_ref, at):
    ext = jnp.concatenate([halo_ref[:, at].astype(F32), v_ref[:, at].astype(F32)], axis=0)
    rows = v_ref.shape[0]
    return [ext[HALO - j : HALO - j + rows] for j in range(CW)]


def tap_rows(w_ref, core, head):
    return w_ref[:, pl.ds(pl.multiple_of(core * WIDE + head * DH, DH), DH)]


def later(rows):
    first = lax.broadcasted_iota(jnp.int32, (rows, rows), 0)
    return first <= lax.broadcasted_iota(jnp.int32, (rows, rows), 1)


def score_kernel(core_ref, q_ref, g_ref, k_ref, state_ref, gc_ref, edge_ref):
    seen = later(q_ref.shape[0])
    for i in range(HALF):
        at = columns(i)
        k = k_ref[:, at]
        score = jnp.where(seen, dot(k, q_ref[:, at], (1, 1)), 0.0).astype(BF16)
        gc = dot(score, g_ref[:, at], (1, 0))
        gc_ref[:, at] = gc.astype(BF16)
        edge = gc[:HALO] - dot(k[:HALO], state_ref[i], (1, 0))
        both = jnp.concatenate([edge[:EDGE], k[:HALO].astype(F32)[:EDGE]], axis=0)
        edge_ref[:, at] = both.astype(BF16)


def conv_kernel(core_ref, k_ref, v_ref, halo_ref, w_ref, c_ref, state_ref):
    for i in range(HALF):
        at = columns(i)
        taps = tap_rows(w_ref, core_ref[0], i)
        parts = lagged(v_ref, halo_ref, at)
        acc = taps[0:1] * parts[0]
        for j in range(1, CW):
            acc = acc + taps[j : j + 1] * parts[j]
        c = acc.astype(BF16)
        c_ref[:, at] = c
        state_ref[i] = dot(k_ref[:, at], c, (0, 0)).astype(BF16)


def turn_kernel(core_ref, q_ref, state_ref, out_ref, done_ref, *, order):
    total = jnp.zeros(q_ref.shape[1:], F32)
    for n in reversed(order):
        out_ref[n, 0] = total.astype(BF16)
        total = total + q_ref[n].astype(F32)
        out_ref[n, 1] = state_ref[n]
    done_ref[...] = jnp.zeros(done_ref.shape, F32)


def attn_kernel(core_ref, q_ref, g_ref, k_ref, c_ref, done_ref, gq_ref, gk_ref):
    seen = later(q_ref.shape[0])
    for i in range(HALF):
        at = columns(i)
        c, g = c_ref[:, at], g_ref[:, at]
        turned = jnp.where(seen, dot(c, g, (1, 1)), 0.0)
        gk_ref[:, at] = dot(turned.astype(BF16), q_ref[:, at], (1, 0)).astype(BF16)
        attn = jnp.where(seen.T, dot(g, c, (1, 1)), 0.0)
        gq_ref[:, at] = dot(attn.astype(BF16), k_ref[:, at], (1, 0)).astype(BF16)


def head_state(read, head, depth):
    parts = DH // depth
    if depth % HALO == 0:
        return jnp.concatenate([read(head * parts + n) for n in range(parts)], axis=0)
    found = [read(head * parts + n).astype(F32) for n in range(parts)]
    return jnp.concatenate(found, axis=0).astype(BF16)


def tap_kernel(
    core_ref, chip_ref, k_ref, gc_ref, v_ref, halo_ref, out_ref, done_ref, taps_ref, *, scale, order
):
    depth = chip_ref.shape[2]
    for i in range(HALF):
        at = columns(i)
        suffix = head_state(lambda n: chip_ref[n, 0], i, depth)
        gc = scale * (gc_ref[:, at].astype(F32) + dot(k_ref[:, at], suffix, (1, 0)))
        for j, part in enumerate(lagged(v_ref, halo_ref, at)):
            row = j * HALF + i
            taps_ref[row : row + 1, :] = jnp.sum(gc * part, axis=0, keepdims=True)
    total = jnp.zeros((depth, DH), F32)
    weights = taps_ref[...].astype(BF16)
    start = out_ref.shape[1] - CW * HALF
    for n in order:
        out_ref[n, :depth] = total.astype(BF16)
        total = total + chip_ref[n, 1].astype(F32)
        out_ref[n, start:] = weights
    done_ref[...] = jnp.zeros(done_ref.shape, F32)


def query_side_kernel(
    core_ref,
    chip_ref,
    k_ref,
    c_ref,
    gk_ref,
    gc_ref,
    edge_ref,
    w_ref,
    done_ref,
    own_ref,
    send_ref,
    *,
    scale,
):
    core = core_ref[0]
    rows = k_ref.shape[0]
    depth = chip_ref.shape[2]
    for i in range(HALF):
        at = columns(i)
        suffix = head_state(lambda n: chip_ref[n, 0], i, depth)
        gk = scale * (gk_ref[:, at].astype(F32) + dot(c_ref[:, at], suffix, (1, 1)))
        gc = scale * (gc_ref[:, at].astype(F32) + dot(k_ref[:, at], suffix, (1, 0)))
        edge = edge_ref[:, at]
        after = dot(edge, suffix, (1, 0))[EDGE:] + edge.astype(F32)[:EDGE]
        ext = jnp.concatenate([gc, scale * after], axis=0)
        taps = tap_rows(w_ref, core, i)
        gv = taps[0:1] * gc
        for j in range(1, CW):
            gv = gv + taps[j : j + 1] * ext[j : j + rows]
        for n, value in enumerate((gk, gv)):
            low, high = value[: rows // 2].astype(BF16), value[rows // 2 :].astype(BF16)
            own_ref[n, :, at] = jnp.where(core == 0, low, high)
            send_ref[n, :, at] = jnp.where(core == 0, high, low)


def key_side_kernel(
    core_ref, chip_ref, g_ref, gq_ref, own_ref, send_ref, taps_ref, *, scale, depth
):
    core = core_ref[0]
    rows = g_ref.shape[0]
    chips, size, _ = chip_ref.shape
    for i in range(HALF):
        at = columns(i)
        prefix = head_state(lambda n: chip_ref[n, :depth], i, depth)
        gq = scale * (gq_ref[:, at].astype(F32) + dot(g_ref[:, at], prefix, (1, 1)))
        low, high = gq[: rows // 2].astype(BF16), gq[rows // 2 :].astype(BF16)
        own_ref[:, at] = jnp.where(core == 0, low, high)
        send_ref[:, at] = jnp.where(core == 0, high, low)
    total = chip_ref[0, size - CW * HALF :].astype(F32)
    for n in range(1, chips):
        total = total + chip_ref[n, size - CW * HALF :].astype(F32)
    taps_ref[...] = total


def join_kernel(core_ref, own_ref, recv_ref, a_ref, b_ref):
    core = core_ref[0]
    for n, ref in enumerate((a_ref, b_ref)):
        ref[:, half_of(core, WIDE)] = own_ref[n]
        ref[:, half_of(1 - core, WIDE)] = recv_ref[n]


def finish_kernel(core_ref, own_ref, recv_ref, taps_ref, far_ref, gq_ref, gw_ref):
    core = core_ref[0]
    gq_ref[:, half_of(core, WIDE)] = own_ref[...]
    gq_ref[:, half_of(1 - core, WIDE)] = recv_ref[...]
    for side, ref in ((core, taps_ref), (1 - core, far_ref)):
        for i in range(HALF):
            at = pl.ds(pl.multiple_of(side * WIDE + i * DH, DH), DH)
            for j in range(CW):
                row = j * HALF + i
                gw_ref[j : j + 1, at] = ref[row : row + 1, :]


def local(queries, keys, values, grad_out, conv_weight):
    rows, width = queries.shape
    lines, line = lax.axis_size("row"), lax.axis_size("col") // 2
    count = 2 * lines * line
    chips = lines * line
    depth = WIDE // chips
    scale = (DH * rows * count) ** (-0.5)
    core = lax.rem(lax.axis_index("col"), 2).astype(jnp.int32).reshape(1)
    listed = [r * line + (z + line // 2) % line for z in range(line) for r in range(lines)]
    groups = [[2 * p + c for p in listed] for c in range(2)]
    order = tuple(listed.index(p) for p in range(chips))

    def swap(value):
        return lax.ppermute(value, AXES, [(d, d ^ 1) for d in range(count)])

    def shifted(value, by):
        pairs = [(d, d + by) for d in range(count) if 0 <= d + by < count]
        return lax.ppermute(value, AXES, pairs)

    def turn(value):
        return lax.all_to_all(value, AXES, 0, 0, axis_index_groups=groups, tiled=True)

    def split(*arrays):
        arrays = [pltpu.with_memory_space_constraint(a, pltpu.HBM) for a in arrays]
        sems = [pltpu.SemaphoreType.DMA((2, 2))]
        return call(split_kernel, (pair, pair), core, arrays, sems, HBM)

    pair = shape((2, rows, WIDE))
    block = shape((2 * rows, WIDE))
    states = shape((HALF, DH, DH))
    edges = shape((HALO, WIDE))
    flag = shape((8, DH), F32)
    qg_own, qg_send = split(queries, grad_out)
    qg_recv = swap(qg_send)
    kv_own, kv_send = split(keys, values)
    kv_recv = swap(kv_send)
    q, g, q_state = call(query_state_kernel, (block, block, states), core, [qg_own, qg_recv])
    q_turned = turn(q_state.reshape(chips, depth, DH))
    k, v, tail = call(gather_kernel, (block, block, edges), core, [kv_own, kv_recv])
    halo = shifted(tail, 2)
    gc, edge = call(score_kernel, (block, edges), core, [q, g, k, q_state])
    c, k_state = call(conv_kernel, (block, states), core, [k, v, halo, conv_weight])
    both, turned = call(
        functools.partial(turn_kernel, order=order),
        (shape((chips, 2, depth, DH)), flag),
        core,
        [q_turned, k_state.reshape(chips, depth, DH)],
    )
    both = turn(both)
    edge = shifted(edge, -2)
    gq, gk = call(attn_kernel, (block, block), core, [q, g, k, c, turned])
    last, tapped = call(
        functools.partial(tap_kernel, scale=scale, order=order),
        (shape((chips, max(depth, HALO) + CW * HALF, DH)), flag),
        core,
        [both, k, gc, v, halo],
        [pltpu.VMEM((CW * HALF, DH), F32)],
    )
    last = turn(last)
    kv_grad, kv_give = call(
        functools.partial(query_side_kernel, scale=scale),
        (pair, pair),
        core,
        [both, k, c, gk, gc, edge, conv_weight, tapped],
    )
    kv_got = swap(kv_give)
    q_grad, q_give, taps = call(
        functools.partial(key_side_kernel, scale=scale, depth=depth),
        (shape((rows, WIDE)), shape((rows, WIDE)), shape((CW * HALF, DH), F32)),
        core,
        [last, g, gq],
    )
    q_got = swap(q_give)
    far = swap(taps)
    full = shape((rows, width))
    grad_keys, grad_values = call(join_kernel, (full, full), core, [kv_grad, kv_got])
    grad_queries, grad_weight = call(
        finish_kernel, (full, shape((CW, width), F32)), core, [q_grad, q_got, taps, far]
    )
    return grad_queries, grad_keys, grad_values, grad_weight


def solution(mesh):
    placed = (
        P(("row", "col"), None),
        P(("row", "col"), None),
        P(("row", "col"), None),
        P(("row", "col"), None),
        P(),
    )
    return jax.shard_map(
        local,
        mesh=mesh,
        in_specs=placed,
        out_specs=(P(("row", "col"), None), P(("row", "col"), None), P(("row", "col"), None), P()),
        check_vma=False,
    )
```

```python
import functools

import jax
import jax.numpy as jnp
from jax import lax
from jax.experimental import pallas as pl
from jax.experimental.pallas import tpu as pltpu
from jax.sharding import PartitionSpec as P

HEADS = 16
DH = 128
CW = 4
HALF = HEADS // 2
WIDE = HALF * DH
EDGE = 8
HALO = 16
AXES = ("row", "col")
F32 = jnp.float32
BF16 = jnp.bfloat16
VMEM = pl.BlockSpec(memory_space=pltpu.VMEM)
SMEM = pl.BlockSpec(memory_space=pltpu.SMEM)
ANY = pl.BlockSpec(memory_space=pl.ANY)
PARAMS = pltpu.CompilerParams(vmem_limit_bytes=16 * 1024 * 1024)


def dot(a, b, over):
    return lax.dot_general(a, b, ((over[:1], over[1:]), ((), ())), preferred_element_type=F32)


def columns(head):
    return pl.ds(head * DH, DH)


def half_of(core, size):
    return pl.ds(pl.multiple_of(core * size, size), size)


def call(kernel, outs, core, arrays, scratch=(), given=None, made=None, aliases={}):
    return pl.pallas_call(
        kernel,
        out_shape=outs,
        in_specs=[SMEM] + (given or [VMEM] * len(arrays)),
        out_specs=made or jax.tree.map(lambda _: VMEM, outs),
        scratch_shapes=scratch,
        input_output_aliases=aliases,
        compiler_params=PARAMS,
    )(core, *arrays)


def shape(dims, dtype=BF16):
    return jax.ShapeDtypeStruct(dims, dtype)


def split_kernel(core_ref, a_ref, b_ref, after_ref, own_ref, send_ref, sems):
    core = core_ref[0]
    copies = []
    for n, ref in enumerate((a_ref, b_ref)):
        for m, (out, side) in enumerate(((send_ref, 1 - core), (own_ref, core))):
            copies.append(
                pltpu.make_async_copy(ref.at[:, half_of(side, WIDE)], out.at[n], sems.at[n, m])
            )
    for copy in copies:
        copy.start()
    for copy in copies:
        copy.wait()


def query_state_kernel(
    core_ref, q_ref, g_ref, keep_ref, give_ref, held_ref, sems
):
    core = core_ref[0]
    copies = [
        pltpu.make_async_copy(ref, held_ref.at[n], sems.at[n])
        for n, ref in enumerate((q_ref, g_ref))
    ]
    for copy in copies:
        copy.start()
    for copy in copies:
        copy.wait()
    for side, out in ((1 - core, give_ref), (core, keep_ref)):
        for i in range(HALF):
            at = pl.ds(pl.multiple_of(side * WIDE + i * DH, DH), DH)
            out[i] = dot(held_ref[0, :, at], held_ref[1, :, at], (0, 0)).astype(BF16)


def add_kernel(core_ref, keep_ref, recv_ref, out_ref, done_ref):
    for i in range(HALF):
        out_ref[i] = (keep_ref[i].astype(F32) + recv_ref[i].astype(F32)).astype(BF16)
    done_ref[...] = jnp.zeros(done_ref.shape, F32)


def gather(core, own_ref, recv_ref, refs):
    rows = own_ref.shape[1]
    for n, ref in enumerate(refs):
        ref[half_of(core, rows), :] = own_ref[n]
        ref[half_of(1 - core, rows), :] = recv_ref[n]


def gather_query_kernel(core_ref, own_ref, recv_ref, k_ref, q_ref, g_ref, edge_ref, far_ref, sem):
    gather(core_ref[0], own_ref, recv_ref, (q_ref, g_ref))
    copy = pltpu.make_async_copy(q_ref, far_ref, sem)
    copy.start()
    first = lax.broadcasted_iota(jnp.int32, (HALO, HALO), 0)
    unseen = first > lax.broadcasted_iota(jnp.int32, (HALO, HALO), 1)
    for i in range(HALF):
        at = columns(i)
        q, g, k = q_ref[:HALO, at], g_ref[:HALO, at], k_ref[:HALO, at]
        score = jnp.where(unseen, dot(k, q, (1, 1)), 0.0).astype(BF16)
        edge = dot(score, g, (1, 0))
        both = jnp.concatenate([-edge[:EDGE], k.astype(F32)[:EDGE]], axis=0)
        edge_ref[:, at] = both.astype(BF16)
    copy.wait()


def gather_key_kernel(core_ref, own_ref, recv_ref, k_ref, v_ref, tail_ref):
    gather(core_ref[0], own_ref, recv_ref, (k_ref, v_ref))
    tail_ref[...] = v_ref[v_ref.shape[0] - HALO :, :]


def lagged(v_ref, halo_ref, at):
    ext = jnp.concatenate([halo_ref[:, at].astype(F32), v_ref[:, at].astype(F32)], axis=0)
    rows = v_ref.shape[0]
    return [ext[HALO - j : HALO - j + rows] for j in range(CW)]


def tap_rows(w_ref, core, head):
    return w_ref[:, pl.ds(pl.multiple_of(core * WIDE + head * DH, DH), DH)]


def later(rows):
    first = lax.broadcasted_iota(jnp.int32, (rows, rows), 0)
    return first <= lax.broadcasted_iota(jnp.int32, (rows, rows), 1)


def add_taps(taps_ref, head, grad, parts):
    for j, part in enumerate(parts):
        row = j * HALF + head
        taps_ref[row : row + 1, :] = jnp.sum(grad * part, axis=0, keepdims=True)


def score_kernel(
    core_ref, q_ref, g_ref, k_ref, v_ref, halo_ref, gc_ref, taps_ref
):
    seen = later(q_ref.shape[0])
    for i in range(HALF):
        at = columns(i)
        k = k_ref[:, at]
        score = jnp.where(seen, dot(k, q_ref[:, at], (1, 1)), 0.0).astype(BF16)
        gc = dot(score, g_ref[:, at], (1, 0))
        gc_ref[:, at] = gc.astype(BF16)
        add_taps(taps_ref, i, gc, lagged(v_ref, halo_ref, at))


def conv_kernel(core_ref, k_ref, v_ref, halo_ref, w_ref, c_ref, state_ref):
    for i in range(HALF):
        at = columns(i)
        taps = tap_rows(w_ref, core_ref[0], i)
        parts = lagged(v_ref, halo_ref, at)
        acc = taps[0:1] * parts[0]
        for j in range(1, CW):
            acc = acc + taps[j : j + 1] * parts[j]
        c = acc.astype(BF16)
        c_ref[:, at] = c
        state_ref[i] = dot(k_ref[:, at], c, (0, 0)).astype(BF16)


def turn_kernel(core_ref, q_ref, state_ref, out_ref, done_ref, *, order):
    total = jnp.zeros(q_ref.shape[1:], F32)
    for n in reversed(order):
        out_ref[n, 0] = total.astype(BF16)
        total = total + q_ref[n].astype(F32)
        out_ref[n, 1] = state_ref[n]
    done_ref[...] = jnp.zeros(done_ref.shape, F32)


def head_state(read, head, depth):
    parts = DH // depth
    if depth % HALO == 0:
        return jnp.concatenate([read(head * parts + n) for n in range(parts)], axis=0)
    found = [read(head * parts + n).astype(F32) for n in range(parts)]
    return jnp.concatenate(found, axis=0).astype(BF16)


def tap_kernel(
    core_ref,
    chip_ref,
    k_ref,
    v_ref,
    halo_ref,
    near_ref,
    edge_ref,
    out_ref,
    done_ref,
    taps_ref,
    *,
    scale,
    order,
):
    depth = chip_ref.shape[2]
    start = out_ref.shape[1] - CW * HALF
    for i in range(HALF):
        at = columns(i)
        suffix = head_state(lambda n: chip_ref[n, 0], i, depth)
        grad = dot(k_ref[:, at], suffix, (1, 0))
        add_taps(taps_ref, i, grad, lagged(v_ref, halo_ref, at))
    weights = (scale * (near_ref[...] + taps_ref[...])).astype(BF16)
    total = jnp.zeros((depth, DH), F32)
    for n in order:
        out_ref[n, :depth] = total.astype(BF16)
        if depth < start:
            out_ref[n, depth:start] = jnp.zeros((start - depth, DH), BF16)
        total = total + chip_ref[n, 1].astype(F32)
        out_ref[n, start:] = weights
    done_ref[...] = jnp.zeros(done_ref.shape, F32)


def query_side_kernel(
    core_ref,
    chip_ref,
    q_ref,
    g_ref,
    k_ref,
    c_ref,
    gc_ref,
    edge_ref,
    w_ref,
    done_ref,
    gk_ref,
    gv_ref,
    send_ref,
    gq_ref,
    own_ref,
    sems,
    *,
    scale,
):
    core = core_ref[0]
    rows = k_ref.shape[0]
    depth = chip_ref.shape[2]
    seen = later(rows)
    for i in range(HALF):
        at = columns(i)
        suffix = head_state(lambda n: chip_ref[n, 0], i, depth)
        c, g, k = c_ref[:, at], g_ref[:, at], k_ref[:, at]
        attn = jnp.where(seen.T, dot(g, c, (1, 1)), 0.0)
        gq_ref[:, at] = dot(attn.astype(BF16), k, (1, 0)).astype(BF16)
        turned = jnp.where(seen, dot(c, g, (1, 1)), 0.0)
        gk = dot(turned.astype(BF16), q_ref[:, at], (1, 0))
        gk = scale * (gk + dot(c, suffix, (1, 1)))
        gc = scale * (gc_ref[:, at].astype(F32) + dot(k, suffix, (1, 0)))
        edge = edge_ref[:, at]
        after = dot(edge, suffix, (1, 0))[EDGE:] + edge.astype(F32)[:EDGE]
        ext = jnp.concatenate([gc, scale * after], axis=0)
        taps = tap_rows(w_ref, core, i)
        gv = taps[0:1] * gc
        for j in range(1, CW):
            gv = gv + taps[j : j + 1] * ext[j : j + rows]
        for n, value in enumerate((gk, gv)):
            low, high = value[: rows // 2].astype(BF16), value[rows // 2 :].astype(BF16)
            own_ref[n, :, at] = jnp.where(core == 0, low, high)
            send_ref[n, :, at] = jnp.where(core == 0, high, low)
    put(own_ref, core, (gk_ref, gv_ref), sems)


def put(half_ref, side, refs, sems):
    copies = [
        pltpu.make_async_copy(half_ref.at[n], ref.at[:, half_of(side, WIDE)], sems.at[n])
        for n, ref in enumerate(refs)
    ]
    for copy in copies:
        copy.start()
    for copy in copies:
        copy.wait()


def key_side_kernel(
    core_ref, chip_ref, g_ref, gq_ref, own_ref, send_ref, taps_ref, *, scale, depth
):
    core = core_ref[0]
    rows = g_ref.shape[0]
    chips, size, _ = chip_ref.shape
    for i in range(HALF):
        at = columns(i)
        prefix = head_state(lambda n: chip_ref[n, :depth], i, depth)
        gq = scale * (gq_ref[:, at].astype(F32) + dot(g_ref[:, at], prefix, (1, 1)))
        low, high = gq[: rows // 2].astype(BF16), gq[rows // 2 :].astype(BF16)
        own_ref[:, at] = jnp.where(core == 0, low, high)
        send_ref[:, at] = jnp.where(core == 0, high, low)
    total = chip_ref[0, size - CW * HALF :].astype(F32)
    for n in range(1, chips):
        total = total + chip_ref[n, size - CW * HALF :].astype(F32)
    taps_ref[...] = total


def join_kernel(core_ref, recv_ref, _, __, gk_ref, gv_ref, sems):
    put(recv_ref, 1 - core_ref[0], (gk_ref, gv_ref), sems)


def finish_kernel(core_ref, own_ref, recv_ref, taps_ref, far_ref, gq_ref, gw_ref):
    core = core_ref[0]
    gq_ref[:, half_of(core, WIDE)] = own_ref[...]
    gq_ref[:, half_of(1 - core, WIDE)] = recv_ref[...]
    for side, ref in ((core, taps_ref), (1 - core, far_ref)):
        for i in range(HALF):
            at = pl.ds(pl.multiple_of(side * WIDE + i * DH, DH), DH)
            for j in range(CW):
                row = j * HALF + i
                gw_ref[j : j + 1, at] = ref[row : row + 1, :]


def local(queries, keys, values, grad_out, conv_weight):
    rows, width = queries.shape
    lines, line = lax.axis_size("row"), lax.axis_size("col") // 2
    count = 2 * lines * line
    chips = lines * line
    depth = WIDE // chips
    scale = (DH * rows * count) ** (-0.5)
    core = lax.rem(lax.axis_index("col"), 2).astype(jnp.int32).reshape(1)
    listed = [r * line + (z + line // 2) % line for z in range(line) for r in range(lines)]
    groups = [[2 * p + c for p in listed] for c in range(2)]
    order = tuple(listed.index(p) for p in range(chips))

    def swap(value):
        return lax.ppermute(value, AXES, [(d, d ^ 1) for d in range(count)])

    def shifted(value, by):
        pairs = [(d, d + by) for d in range(count) if 0 <= d + by < count]
        return lax.ppermute(value, AXES, pairs)

    def turn(value):
        return lax.all_to_all(value, AXES, 0, 0, axis_index_groups=groups, tiled=True)

    pair = shape((2, rows, WIDE))
    block = shape((2 * rows, WIDE))
    far_block = pltpu.HBM((2 * rows, WIDE), BF16)
    states = shape((HALF, DH, DH))
    edges = shape((HALO, WIDE))
    flag = shape((8, DH), F32)
    dma = pltpu.SemaphoreType.DMA
    queries, grad_out, keys, values = (
        pltpu.with_memory_space_constraint(a, pltpu.HBM)
        for a in (queries, grad_out, keys, values)
    )
    q_keep, q_give = call(
        query_state_kernel,
        (states, states),
        core,
        [queries, grad_out],
        [pltpu.VMEM((2, rows, width), BF16), dma((2,))],
        [ANY] * 2,
    )
    q_recv = swap(q_give)
    kv_own, kv_send = call(
        split_kernel,
        (pair, pair),
        core,
        [keys, values, q_keep],
        [dma((2, 2))],
        [ANY, ANY, VMEM],
    )
    kv_recv = swap(kv_send)
    q_sent, added = call(
        add_kernel,
        (states, flag),
        core,
        [q_keep, q_recv],
    )
    q_turned = turn(q_sent.reshape(chips, depth, DH))
    qg_own, qg_send = call(
        split_kernel,
        (pair, pair),
        core,
        [queries, grad_out, added],
        [dma((2, 2))],
        [ANY, ANY, VMEM],
    )
    qg_recv = swap(qg_send)
    k, v, tail = call(gather_key_kernel, (block, block, edges), core, [kv_own, kv_recv])
    halo = shifted(tail, 2)
    q, g, edge, q_far = call(
        gather_query_kernel,
        (block, block, edges, far_block),
        core,
        [qg_own, qg_recv, k],
        [dma(())],
        made=(VMEM, VMEM, VMEM, ANY),
    )
    c, k_state = call(conv_kernel, (block, states), core, [k, v, halo, conv_weight])
    both, turned = call(
        functools.partial(turn_kernel, order=order),
        (shape((chips, 2, depth, DH)), flag),
        core,
        [q_turned, k_state.reshape(chips, depth, DH)],
    )
    both = turn(both)
    gc, taps = call(
        score_kernel, (far_block, shape((CW * HALF, DH), F32)), core, [q, g, k, v, halo]
    )
    edge = shifted(edge, -2)
    last, tapped = call(
        functools.partial(tap_kernel, scale=scale, order=order),
        (shape((chips, max(depth, HALO) + CW * HALF, DH)), flag),
        core,
        [both, k, v, halo, taps, edge],
        [pltpu.VMEM((CW * HALF, DH), F32)],
    )
    last = turn(last)
    full = shape((rows, width))
    grad_keys, grad_values, kv_give, gq = call(
        functools.partial(query_side_kernel, scale=scale),
        (full, full, pair, block),
        core,
        [both, q_far, g, k, c, gc, edge, conv_weight, tapped],
        [pltpu.VMEM((2, rows, WIDE), BF16), dma((2,))],
        made=(ANY, ANY, VMEM, VMEM),
    )
    kv_got = swap(kv_give)
    q_grad, q_give, taps = call(
        functools.partial(key_side_kernel, scale=scale, depth=depth),
        (shape((rows, WIDE)), shape((rows, WIDE)), shape((CW * HALF, DH), F32)),
        core,
        [last, g, gq],
    )
    q_got = swap(q_give)
    far = swap(taps)
    grad_keys, grad_values = call(
        join_kernel,
        (full, full),
        core,
        [kv_got, grad_keys, grad_values],
        [dma((2,))],
        [VMEM, ANY, ANY],
        (ANY, ANY),
        {2: 0, 3: 1},
    )
    grad_queries, grad_weight = call(
        finish_kernel, (full, shape((CW, width), F32)), core, [q_grad, q_got, taps, far]
    )
    return grad_queries, grad_keys, grad_values, grad_weight


def solution(mesh):
    placed = (
        P(("row", "col"), None),
        P(("row", "col"), None),
        P(("row", "col"), None),
        P(("row", "col"), None),
        P(),
    )
    return jax.shard_map(
        local,
        mesh=mesh,
        in_specs=placed,
        out_specs=(P(("row", "col"), None), P(("row", "col"), None), P(("row", "col"), None), P()),
        check_vma=False,
    )
```

```python
import functools

import jax
import jax.numpy as jnp
from jax import lax
from jax.experimental import pallas as pl
from jax.experimental.pallas import tpu as pltpu
from jax.sharding import PartitionSpec as P

HEADS = 16
DH = 128
CW = 4
HALF = HEADS // 2
WIDE = HALF * DH
EDGE = 8
HALO = 16
AXES = ("row", "col")
F32 = jnp.float32
BF16 = jnp.bfloat16
VMEM = pl.BlockSpec(memory_space=pltpu.VMEM)
SMEM = pl.BlockSpec(memory_space=pltpu.SMEM)
ANY = pl.BlockSpec(memory_space=pl.ANY)
PARAMS = pltpu.CompilerParams(vmem_limit_bytes=16 * 1024 * 1024)


def dot(a, b, over):
    return lax.dot_general(a, b, ((over[:1], over[1:]), ((), ())), preferred_element_type=F32)


def columns(head):
    return pl.ds(head * DH, DH)


def half_of(core, size):
    return pl.ds(pl.multiple_of(core * size, size), size)


def call(kernel, outs, core, arrays, scratch=(), given=None, made=None, aliases={}):
    return pl.pallas_call(
        kernel,
        out_shape=outs,
        in_specs=[SMEM] + (given or [VMEM] * len(arrays)),
        out_specs=made or jax.tree.map(lambda _: VMEM, outs),
        scratch_shapes=scratch,
        input_output_aliases=aliases,
        compiler_params=PARAMS,
    )(core, *arrays)


def shape(dims, dtype=BF16):
    return jax.ShapeDtypeStruct(dims, dtype)


def split_kernel(core_ref, a_ref, b_ref, after_ref, own_ref, send_ref, sems):
    core = core_ref[0]
    copies = []
    for n, ref in enumerate((a_ref, b_ref)):
        for m, (out, side) in enumerate(((send_ref, 1 - core), (own_ref, core))):
            copies.append(
                pltpu.make_async_copy(ref.at[:, half_of(side, WIDE)], out.at[n], sems.at[n, m])
            )
    for copy in copies:
        copy.start()
    for copy in copies:
        copy.wait()


def query_state_kernel(
    core_ref, q_ref, g_ref, keep_ref, give_ref, held_ref, sems
):
    core = core_ref[0]
    copies = [
        pltpu.make_async_copy(ref, held_ref.at[n], sems.at[n])
        for n, ref in enumerate((q_ref, g_ref))
    ]
    for copy in copies:
        copy.start()
    for copy in copies:
        copy.wait()
    for side, out in ((1 - core, give_ref), (core, keep_ref)):
        for i in range(HALF):
            at = pl.ds(pl.multiple_of(side * WIDE + i * DH, DH), DH)
            out[i] = dot(held_ref[0, :, at], held_ref[1, :, at], (0, 0)).astype(BF16)


def add_kernel(core_ref, keep_ref, recv_ref, out_ref, done_ref):
    for i in range(HALF):
        out_ref[i] = (keep_ref[i].astype(F32) + recv_ref[i].astype(F32)).astype(BF16)
    done_ref[...] = jnp.zeros(done_ref.shape, F32)


def gather(core, own_ref, recv_ref, refs):
    rows = own_ref.shape[1]
    for n, ref in enumerate(refs):
        ref[half_of(core, rows), :] = own_ref[n]
        ref[half_of(1 - core, rows), :] = recv_ref[n]


def gather_query_kernel(core_ref, own_ref, recv_ref, k_ref, q_ref, g_ref, edge_ref, far_ref, sem):
    gather(core_ref[0], own_ref, recv_ref, (q_ref, g_ref))
    copy = pltpu.make_async_copy(q_ref, far_ref, sem)
    copy.start()
    first = lax.broadcasted_iota(jnp.int32, (HALO, HALO), 0)
    unseen = first > lax.broadcasted_iota(jnp.int32, (HALO, HALO), 1)
    for i in range(HALF):
        at = columns(i)
        q, g, k = q_ref[:HALO, at], g_ref[:HALO, at], k_ref[:HALO, at]
        score = jnp.where(unseen, dot(k, q, (1, 1)), 0.0).astype(BF16)
        edge = dot(score, g, (1, 0))
        both = jnp.concatenate([-edge[:EDGE], k.astype(F32)[:EDGE]], axis=0)
        edge_ref[:, at] = both.astype(BF16)
    copy.wait()


def gather_key_kernel(core_ref, own_ref, recv_ref, k_ref, v_ref, tail_ref):
    gather(core_ref[0], own_ref, recv_ref, (k_ref, v_ref))
    tail_ref[...] = v_ref[v_ref.shape[0] - HALO :, :]


def lagged(v_ref, halo_ref, at):
    ext = jnp.concatenate([halo_ref[:, at].astype(F32), v_ref[:, at].astype(F32)], axis=0)
    rows = v_ref.shape[0]
    return [ext[HALO - j : HALO - j + rows] for j in range(CW)]


def tap_rows(w_ref, core, head):
    return w_ref[:, pl.ds(pl.multiple_of(core * WIDE + head * DH, DH), DH)]


def later(rows):
    first = lax.broadcasted_iota(jnp.int32, (rows, rows), 0)
    return first <= lax.broadcasted_iota(jnp.int32, (rows, rows), 1)


def tap_states(wide_ref, head, k, parts):
    for j, part in enumerate(parts):
        wide_ref[head, j] = dot(k, part.astype(BF16), (0, 0)).astype(BF16)


def add_taps(taps_ref, head, grad, parts):
    for j, part in enumerate(parts):
        row = j * HALF + head
        taps_ref[row : row + 1, :] = jnp.sum(grad * part, axis=0, keepdims=True)


def score_kernel(
    core_ref, q_ref, g_ref, k_ref, v_ref, halo_ref, gc_ref, taps_ref, wide_ref
):
    seen = later(q_ref.shape[0])
    for i in range(HALF):
        at = columns(i)
        k = k_ref[:, at]
        score = jnp.where(seen, dot(k, q_ref[:, at], (1, 1)), 0.0).astype(BF16)
        gc = dot(score, g_ref[:, at], (1, 0))
        gc_ref[:, at] = gc.astype(BF16)
        parts = lagged(v_ref, halo_ref, at)
        add_taps(taps_ref, i, gc, parts)
        tap_states(wide_ref, i, k, parts)


def convolved(w_ref, core, head, parts):
    taps = tap_rows(w_ref, core, head)
    acc = taps[0:1] * parts[0]
    for j in range(1, CW):
        acc = acc + taps[j : j + 1] * parts[j]
    return acc


def conv_kernel(core_ref, k_ref, v_ref, w_ref, c_ref, state_ref):
    rows = v_ref.shape[0]
    body = lax.broadcasted_iota(jnp.int32, (rows, DH), 0) >= HALO
    for i in range(HALF):
        at = columns(i)
        v = v_ref[:, at].astype(F32)
        ext = jnp.concatenate([jnp.zeros((HALO, DH), F32), v], axis=0)
        parts = [ext[HALO - j : HALO - j + rows] for j in range(CW)]
        c = jnp.where(body, convolved(w_ref, core_ref[0], i, parts), 0.0).astype(BF16)
        c_ref[:, at] = c
        state_ref[i] = dot(k_ref[:, at], c, (0, 0))


def turn_kernel(
    core_ref,
    q_ref,
    state_ref,
    k_ref,
    v_ref,
    halo_ref,
    w_ref,
    out_ref,
    head_ref,
    done_ref,
    *,
    order,
):
    depth = q_ref.shape[1]
    for i in range(HALF):
        at = columns(i)
        start = v_ref[:HALO, at].astype(F32)
        ext = jnp.concatenate([halo_ref[:, at].astype(F32), start], axis=0)
        parts = [ext[HALO - j : 2 * HALO - j] for j in range(CW)]
        c = convolved(w_ref, core_ref[0], i, parts).astype(BF16)
        head_ref[:, at] = c
        state = state_ref[i] + dot(k_ref[:HALO, at], c, (0, 0))
        for n in range(DH // depth):
            part = state[n * depth : (n + 1) * depth].astype(BF16)
            out_ref[i * (DH // depth) + n, 1] = part
    total = jnp.zeros(q_ref.shape[1:], F32)
    for n in reversed(order):
        out_ref[n, 0] = total.astype(BF16)
        total = total + q_ref[n].astype(F32)
    done_ref[...] = jnp.zeros(done_ref.shape, F32)


def head_state(read, head, depth):
    parts = DH // depth
    if depth % HALO == 0:
        return jnp.concatenate([read(head * parts + n) for n in range(parts)], axis=0)
    found = [read(head * parts + n).astype(F32) for n in range(parts)]
    return jnp.concatenate(found, axis=0).astype(BF16)


def tap_kernel(
    core_ref,
    chip_ref,
    wide_ref,
    near_ref,
    edge_ref,
    out_ref,
    done_ref,
    taps_ref,
    hold_ref,
    weights_ref,
    sems,
    *,
    scale,
    places,
):
    depth, size = chip_ref.shape[2], hold_ref.shape[1]
    total = jnp.zeros((depth, DH), F32)
    for n, slot in places:
        hold_ref[slot, :depth] = total.astype(BF16)
        if depth < size:
            hold_ref[slot, depth:] = jnp.zeros((size - depth, DH), BF16)
        total = total + chip_ref[n, 1].astype(F32)
    states = pltpu.make_async_copy(hold_ref, out_ref.at[:, pl.ds(0, size)], sems.at[0])
    states.start()
    for i in range(HALF):
        suffix = head_state(lambda n: chip_ref[n, 0], i, depth).astype(F32)
        add_taps(taps_ref, i, suffix, [wide_ref[i, j].astype(F32) for j in range(CW)])
    weights = (scale * (near_ref[...] + taps_ref[...])).astype(BF16)
    for n in range(weights_ref.shape[0]):
        weights_ref[n] = weights
    place = out_ref.at[:, pl.ds(size, CW * HALF)]
    weights = pltpu.make_async_copy(weights_ref, place, sems.at[1])
    weights.start()
    done_ref[...] = jnp.zeros(done_ref.shape, F32)
    states.wait()
    weights.wait()


def query_side_kernel(
    core_ref,
    chip_ref,
    k_ref,
    g_ref,
    head_ref,
    edge_ref,
    w_ref,
    done_ref,
    c_ref,
    gc_ref,
    q_ref,
    gk_ref,
    gv_ref,
    send_ref,
    gq_ref,
    own_ref,
    hold_ref,
    sems,
    fetch_sems,
    *,
    scale,
):
    core = core_ref[0]
    rows = k_ref.shape[0]
    depth = chip_ref.shape[2]
    seen = later(rows)
    fetches = [
        pltpu.make_async_copy(ref, hold_ref.at[n], fetch_sems.at[n])
        for n, ref in enumerate((c_ref, q_ref, gc_ref))
    ]
    for fetch in fetches:
        fetch.start()
    for fetch in fetches:
        fetch.wait()
    for i in range(HALF):
        at = columns(i)
        suffix = head_state(lambda n: chip_ref[n, 0], i, depth)
        c = jnp.concatenate([head_ref[:, at], hold_ref[0, HALO:, at]], axis=0)
        g, k = g_ref[:, at], k_ref[:, at]
        attn = jnp.where(seen.T, dot(g, c, (1, 1)), 0.0)
        gq_ref[:, at] = dot(attn.astype(BF16), k, (1, 0)).astype(BF16)
        turned = jnp.where(seen, dot(c, g, (1, 1)), 0.0)
        gk = dot(turned.astype(BF16), hold_ref[1, :, at], (1, 0))
        gk = scale * (gk + dot(c, suffix, (1, 1)))
        gc = scale * (hold_ref[2, :, at].astype(F32) + dot(k, suffix, (1, 0)))
        edge = edge_ref[:, at]
        after = dot(edge, suffix, (1, 0))[EDGE:] + edge.astype(F32)[:EDGE]
        ext = jnp.concatenate([gc, scale * after], axis=0)
        taps = tap_rows(w_ref, core, i)
        gv = taps[0:1] * gc
        for j in range(1, CW):
            gv = gv + taps[j : j + 1] * ext[j : j + rows]
        for n, value in enumerate((gk, gv)):
            low, high = value[: rows // 2].astype(BF16), value[rows // 2 :].astype(BF16)
            own_ref[n, :, at] = jnp.where(core == 0, low, high)
            send_ref[n, :, at] = jnp.where(core == 0, high, low)
    put(own_ref, core, (gk_ref, gv_ref), sems)


def put(half_ref, side, refs, sems):
    copies = [
        pltpu.make_async_copy(half_ref.at[n], ref.at[:, half_of(side, WIDE)], sems.at[n])
        for n, ref in enumerate(refs)
    ]
    for copy in copies:
        copy.start()
    for copy in copies:
        copy.wait()


def key_side_kernel(
    core_ref, chip_ref, g_ref, gq_ref, own_ref, send_ref, taps_ref, *, scale, depth, slots
):
    core = core_ref[0]
    rows = g_ref.shape[0]
    chips, size, _ = chip_ref.shape
    for i in range(HALF):
        at = columns(i)
        prefix = head_state(lambda n: chip_ref[slots[n], :depth], i, depth)
        gq = scale * (gq_ref[:, at].astype(F32) + dot(g_ref[:, at], prefix, (1, 1)))
        low, high = gq[: rows // 2].astype(BF16), gq[rows // 2 :].astype(BF16)
        own_ref[:, at] = jnp.where(core == 0, low, high)
        send_ref[:, at] = jnp.where(core == 0, high, low)
    total = chip_ref[0, size - CW * HALF :].astype(F32)
    for n in range(1, chips):
        total = total + chip_ref[n, size - CW * HALF :].astype(F32)
    taps_ref[...] = total


def join_kernel(core_ref, recv_ref, _, __, gk_ref, gv_ref, sems):
    put(recv_ref, 1 - core_ref[0], (gk_ref, gv_ref), sems)


def finish_kernel(
    core_ref, own_ref, recv_ref, taps_ref, far_ref, gq_ref, gw_ref, hold_ref, sems
):
    core = core_ref[0]
    copies = [
        pltpu.make_async_copy(ref, gq_ref.at[:, half_of(side, WIDE)], sems.at[n])
        for n, (side, ref) in enumerate(((1 - core, recv_ref), (core, own_ref)))
    ]
    for copy in copies:
        copy.start()
    for side, ref in ((core, taps_ref), (1 - core, far_ref)):
        for i in range(HALF):
            at = pl.ds(pl.multiple_of(side * WIDE + i * DH, DH), DH)
            for j in range(CW):
                row = j * HALF + i
                hold_ref[j : j + 1, at] = ref[row : row + 1, :]
    copies.append(pltpu.make_async_copy(hold_ref, gw_ref, sems.at[2]))
    copies[-1].start()
    for copy in copies:
        copy.wait()


def local(queries, keys, values, grad_out, conv_weight):
    rows, width = queries.shape
    lines, line = lax.axis_size("row"), lax.axis_size("col") // 2
    count = 2 * lines * line
    chips = lines * line
    depth = WIDE // chips
    scale = (DH * rows * count) ** (-0.5)
    core = lax.rem(lax.axis_index("col"), 2).astype(jnp.int32).reshape(1)
    half = line // 2
    along = [z for n in range(half) for z in (half + n, n)]
    listed = [r * line + z for r in reversed(range(lines)) for z in along]
    groups = [[2 * p + c for p in listed] for c in range(2)]
    order = tuple(listed.index(p) for p in range(chips))
    final = listed
    final_groups = [[2 * p + c for p in final] for c in range(2)]
    places = tuple((order[p], final.index(p)) for p in range(chips))
    slots = tuple(final.index(p) for p in listed)

    def swap(value):
        return lax.ppermute(value, AXES, [(d, d ^ 1) for d in range(count)])

    def shifted(value, by):
        pairs = [(d, d + by) for d in range(count) if 0 <= d + by < count]
        return lax.ppermute(value, AXES, pairs)

    def turn(value, groups):
        return lax.all_to_all(value, AXES, 0, 0, axis_index_groups=groups, tiled=True)

    pair = shape((2, rows, WIDE))
    block = shape((2 * rows, WIDE))
    far_block = pltpu.HBM((2 * rows, WIDE), BF16)
    states = shape((HALF, DH, DH))
    edges = shape((HALO, WIDE))
    flag = shape((8, DH), F32)
    dma = pltpu.SemaphoreType.DMA
    padded = max(depth, HALO)

    def in_hbm(value):
        return pltpu.with_memory_space_constraint(value, pltpu.HBM)

    queries, grad_out, keys, values = map(in_hbm, (queries, grad_out, keys, values))
    q_keep, q_give = call(
        query_state_kernel,
        (states, states),
        core,
        [queries, grad_out],
        [pltpu.VMEM((2, rows, width), BF16), dma((2,))],
        [ANY] * 2,
    )
    q_recv = swap(q_give)
    kv_own, kv_send = call(
        split_kernel,
        (pair, pair),
        core,
        [keys, values, q_keep],
        [dma((2, 2))],
        [ANY, ANY, VMEM],
    )
    kv_recv = swap(kv_send)
    q_sent, added = call(
        add_kernel,
        (states, flag),
        core,
        [q_keep, q_recv],
    )
    q_turned = turn(q_sent.reshape(chips, depth, DH), groups)
    qg_own, qg_send = call(
        split_kernel,
        (pair, pair),
        core,
        [queries, grad_out, added],
        [dma((2, 2))],
        [ANY, ANY, VMEM],
    )
    qg_recv = swap(qg_send)
    k, v, tail = call(gather_key_kernel, (block, block, edges), core, [kv_own, kv_recv])
    halo = shifted(tail, 2)
    q, g, edge, q_far = call(
        gather_query_kernel,
        (block, block, edges, far_block),
        core,
        [qg_own, qg_recv, k],
        [dma(())],
        made=(VMEM, VMEM, VMEM, ANY),
    )
    c, k_state = call(
        conv_kernel,
        (far_block, shape((HALF, DH, DH), F32)),
        core,
        [k, v, conv_weight],
    )
    both, c_head, turned = call(
        functools.partial(turn_kernel, order=order),
        (shape((chips, 2, depth, DH)), edges, flag),
        core,
        [q_turned, k_state, k, v, halo, conv_weight],
    )
    both = turn(both, groups)
    gc, taps, wide = call(
        score_kernel,
        (far_block, shape((CW * HALF, DH), F32), shape((HALF, CW, DH, DH))),
        core,
        [q, g, k, v, halo]
    )
    edge = shifted(edge, -2)
    last, tapped = call(
        functools.partial(tap_kernel, scale=scale, places=places),
        (pltpu.HBM((chips, padded + CW * HALF, DH), BF16), flag),
        core,
        [both, wide, taps, edge],
        [
            pltpu.VMEM((CW * HALF, DH), F32),
            pltpu.VMEM((chips, padded, DH), BF16),
            pltpu.VMEM((chips, CW * HALF, DH), BF16),
            dma((2,)),
        ],
        made=(ANY, VMEM),
    )
    last = turn(last, final_groups)
    full = shape((rows, width))
    grad_keys, grad_values, kv_give, gq = call(
        functools.partial(query_side_kernel, scale=scale),
        (full, full, pair, block),
        core,
        [both, k, g, c_head, edge, conv_weight, tapped, *map(in_hbm, (c, gc, q_far))],
        [pltpu.VMEM((2, rows, WIDE), BF16), pltpu.VMEM((3, 2 * rows, WIDE), BF16)]
        + [dma((2,)), dma((3,))],
        [VMEM] * 7 + [ANY] * 3,
        (ANY, ANY, VMEM, VMEM),
    )
    kv_got = swap(kv_give)
    q_grad, q_give, taps = call(
        functools.partial(key_side_kernel, scale=scale, depth=depth, slots=slots),
        (shape((rows, WIDE)), shape((rows, WIDE)), shape((CW * HALF, DH), F32)),
        core,
        [last, g, gq],
    )
    q_got = swap(q_give)
    far = swap(taps)
    grad_keys, grad_values = call(
        join_kernel,
        (full, full),
        core,
        [kv_got, grad_keys, grad_values],
        [dma((2,))],
        [VMEM, ANY, ANY],
        (ANY, ANY),
        {2: 0, 3: 1},
    )
    grad_queries, grad_weight = call(
        finish_kernel,
        (full, shape((CW, width), F32)),
        core,
        [q_grad, q_got, taps, far],
        [pltpu.VMEM((CW, width), F32), dma((3,))],
        made=(ANY, ANY),
    )
    return grad_queries, grad_keys, grad_values, grad_weight


def solution(mesh):
    placed = (
        P(("row", "col"), None),
        P(("row", "col"), None),
        P(("row", "col"), None),
        P(("row", "col"), None),
        P(),
    )
    return jax.shard_map(
        local,
        mesh=mesh,
        in_specs=placed,
        out_specs=(P(("row", "col"), None), P(("row", "col"), None), P(("row", "col"), None), P()),
        check_vma=False,
    )
```

```python
import functools

import jax
import jax.numpy as jnp
from jax import lax
from jax.experimental import pallas as pl
from jax.experimental.pallas import tpu as pltpu
from jax.sharding import PartitionSpec as P

HEADS = 16
DH = 128
CW = 4
HALF = HEADS // 2
WIDE = HALF * DH
EDGE = 4
TILE = 8
HALO = 16
AXES = ("row", "col")
F32 = jnp.float32
BF16 = jnp.bfloat16
VMEM = pl.BlockSpec(memory_space=pltpu.VMEM)
SMEM = pl.BlockSpec(memory_space=pltpu.SMEM)
ANY = pl.BlockSpec(memory_space=pl.ANY)
PARAMS = pltpu.CompilerParams(vmem_limit_bytes=16 * 1024 * 1024)


def dot(a, b, over):
    return lax.dot_general(a, b, ((over[:1], over[1:]), ((), ())), preferred_element_type=F32)


def columns(head):
    return pl.ds(head * DH, DH)


def half_of(core, size):
    return pl.ds(pl.multiple_of(core * size, size), size)


def call(kernel, outs, core, arrays, scratch=(), given=None, made=None, aliases={}):
    return pl.pallas_call(
        kernel,
        out_shape=outs,
        in_specs=[SMEM] + (given or [VMEM] * len(arrays)),
        out_specs=made or jax.tree.map(lambda _: VMEM, outs),
        scratch_shapes=scratch,
        input_output_aliases=aliases,
        compiler_params=PARAMS,
    )(core, *arrays)


def shape(dims, dtype=BF16):
    return jax.ShapeDtypeStruct(dims, dtype)


def split_key_kernel(
    core_ref, k_ref, v_ref, q_ref, g_ref, after_ref, own_ref, send_ref, sems
):
    core = core_ref[0]
    rows = k_ref.shape[0]
    copies = []
    for n, refs in enumerate(((k_ref, q_ref), (v_ref, g_ref))):
        for m, (out, side) in enumerate(((send_ref, 1 - core), (own_ref, core))):
            for e, (ref, first, size) in enumerate(zip(refs, (0, rows), (rows, HALO))):
                part = ref.at[pl.ds(0, size), half_of(side, WIDE)]
                place = out.at[n, pl.ds(first, size)]
                copies.append(pltpu.make_async_copy(part, place, sems.at[n, m, e]))
    for copy in copies:
        copy.start()
    for copy in copies:
        copy.wait()


def split_kernel(core_ref, a_ref, b_ref, after_ref, own_ref, send_ref, sems):
    core = core_ref[0]
    copies = []
    for n, ref in enumerate((a_ref, b_ref)):
        for m, (out, side) in enumerate(((send_ref, 1 - core), (own_ref, core))):
            copies.append(
                pltpu.make_async_copy(ref.at[:, half_of(side, WIDE)], out.at[n], sems.at[n, m])
            )
    for copy in copies:
        copy.start()
    for copy in copies:
        copy.wait()


def query_state_kernel(
    core_ref, q_ref, g_ref, keep_ref, give_ref, held_ref, sems
):
    core = core_ref[0]
    copies = [
        pltpu.make_async_copy(ref, held_ref.at[n], sems.at[n])
        for n, ref in enumerate((q_ref, g_ref))
    ]
    for copy in copies:
        copy.start()
    for copy in copies:
        copy.wait()
    for side, out in ((1 - core, give_ref), (core, keep_ref)):
        for i in range(HALF):
            at = pl.ds(pl.multiple_of(side * WIDE + i * DH, DH), DH)
            out[i] = dot(held_ref[0, :, at], held_ref[1, :, at], (0, 0)).astype(BF16)


def add_kernel(core_ref, keep_ref, recv_ref, out_ref, done_ref):
    for i in range(HALF):
        out_ref[i] = (keep_ref[i].astype(F32) + recv_ref[i].astype(F32)).astype(BF16)
    done_ref[...] = jnp.zeros(done_ref.shape, F32)


def gather(core, own_ref, recv_ref, refs):
    for n, ref in enumerate(refs):
        rows = ref.shape[0] // 2
        ref[half_of(core, rows), :] = own_ref[n, :rows]
        ref[half_of(1 - core, rows), :] = recv_ref[n, :rows]


def gather_query_kernel(core_ref, own_ref, recv_ref, q_ref, g_ref, far_ref, sem):
    gather(core_ref[0], own_ref, recv_ref, (q_ref, g_ref))
    copy = pltpu.make_async_copy(q_ref, far_ref, sem)
    copy.start()
    copy.wait()


def gather_key_kernel(core_ref, own_ref, recv_ref, k_ref, v_ref, tail_ref, edge_ref):
    core = core_ref[0]
    gather(core, own_ref, recv_ref, (k_ref, v_ref))
    rows = k_ref.shape[0]
    tails, edges = [], []
    first = lax.broadcasted_iota(jnp.int32, (HALO, HALO), 0)
    unseen = first > lax.broadcasted_iota(jnp.int32, (HALO, HALO), 1)
    for i in range(HALF):
        at = columns(i)
        q, g = (
            jnp.where(core == 0, own_ref[n, rows // 2 :, at], recv_ref[n, rows // 2 :, at])
            for n in range(2)
        )
        k = k_ref[:HALO, at]
        score = jnp.where(unseen, dot(k, q, (1, 1)), 0.0).astype(BF16)
        edges += [-dot(score, g, (1, 0))[:EDGE], k.astype(F32)[:EDGE]]
        tails.append(v_ref[rows - HALO :, at].astype(F32)[HALO - EDGE :])
    tail_ref[...] = jnp.concatenate(tails, axis=0).astype(BF16)
    edge_ref[...] = jnp.concatenate(edges, axis=0).astype(BF16)


def lagged(v, halo_ref, head):
    halo = halo_ref[...].astype(F32)[head * EDGE : (head + 1) * EDGE]
    ext = jnp.concatenate([jnp.zeros((TILE - EDGE, DH), F32), halo, v.astype(F32)], axis=0)
    return [ext[TILE - j : TILE - j + v.shape[0]] for j in range(CW)]


def tap_rows(w_ref, core, head):
    return w_ref[:, pl.ds(pl.multiple_of(core * WIDE + head * DH, DH), DH)]


def later(rows):
    first = lax.broadcasted_iota(jnp.int32, (rows, rows), 0)
    return first <= lax.broadcasted_iota(jnp.int32, (rows, rows), 1)


def tap_states(wide_ref, head, k, parts):
    for j, part in enumerate(parts):
        wide_ref[head, j] = dot(k, part.astype(BF16), (0, 0)).astype(BF16)


def add_taps(taps_ref, head, grad, parts):
    for j, part in enumerate(parts):
        row = j * HALF + head
        taps_ref[row : row + 1, :] = jnp.sum(grad * part, axis=0, keepdims=True)


def score_kernel(
    core_ref, q_ref, g_ref, k_ref, v_ref, halo_ref, gc_ref, taps_ref, wide_ref
):
    seen = later(q_ref.shape[0])
    for i in range(HALF):
        at = columns(i)
        k = k_ref[:, at]
        score = jnp.where(seen, dot(k, q_ref[:, at], (1, 1)), 0.0).astype(BF16)
        gc = dot(score, g_ref[:, at], (1, 0))
        gc_ref[:, at] = gc.astype(BF16)
        parts = lagged(v_ref[:, at], halo_ref, i)
        add_taps(taps_ref, i, gc, parts)
        tap_states(wide_ref, i, k, parts)


def convolved(w_ref, core, head, parts):
    taps = tap_rows(w_ref, core, head)
    acc = taps[0:1] * parts[0]
    for j in range(1, CW):
        acc = acc + taps[j : j + 1] * parts[j]
    return acc


def conv_kernel(core_ref, k_ref, v_ref, w_ref, c_ref, state_ref):
    rows = v_ref.shape[0]
    body = lax.broadcasted_iota(jnp.int32, (rows, DH), 0) >= HALO
    for i in range(HALF):
        at = columns(i)
        v = v_ref[:, at].astype(F32)
        ext = jnp.concatenate([jnp.zeros((HALO, DH), F32), v], axis=0)
        parts = [ext[HALO - j : HALO - j + rows] for j in range(CW)]
        c = jnp.where(body, convolved(w_ref, core_ref[0], i, parts), 0.0).astype(BF16)
        c_ref[:, at] = c
        state_ref[i] = dot(k_ref[:, at], c, (0, 0))


def turn_kernel(
    core_ref,
    q_ref,
    state_ref,
    k_ref,
    v_ref,
    halo_ref,
    w_ref,
    out_ref,
    head_ref,
    done_ref,
    *,
    order,
):
    depth = q_ref.shape[1]
    for i in range(HALF):
        at = columns(i)
        parts = lagged(v_ref[:HALO, at], halo_ref, i)
        c = convolved(w_ref, core_ref[0], i, parts).astype(BF16)
        head_ref[:, at] = c
        state = state_ref[i] + dot(k_ref[:HALO, at], c, (0, 0))
        for n in range(DH // depth):
            part = state[n * depth : (n + 1) * depth].astype(BF16)
            out_ref[i * (DH // depth) + n, 1] = part
    total = jnp.zeros(q_ref.shape[1:], F32)
    for n in reversed(order):
        out_ref[n, 0] = total.astype(BF16)
        total = total + q_ref[n].astype(F32)
    done_ref[...] = jnp.zeros(done_ref.shape, F32)


def head_state(read, head, depth):
    parts = DH // depth
    if depth % HALO == 0:
        return jnp.concatenate([read(head * parts + n) for n in range(parts)], axis=0)
    found = [read(head * parts + n).astype(F32) for n in range(parts)]
    return jnp.concatenate(found, axis=0).astype(BF16)


def tap_kernel(
    core_ref,
    chip_ref,
    wide_ref,
    near_ref,
    edge_ref,
    out_ref,
    done_ref,
    taps_ref,
    hold_ref,
    weights_ref,
    sems,
    *,
    scale,
    places,
):
    depth, size = chip_ref.shape[2], hold_ref.shape[1]
    total = jnp.zeros((depth, DH), F32)
    for n, slot in places:
        hold_ref[slot, :depth] = total.astype(BF16)
        if depth < size:
            hold_ref[slot, depth:] = jnp.zeros((size - depth, DH), BF16)
        total = total + chip_ref[n, 1].astype(F32)
    states = pltpu.make_async_copy(hold_ref, out_ref.at[:, pl.ds(0, size)], sems.at[0])
    states.start()
    for i in range(HALF):
        suffix = head_state(lambda n: chip_ref[n, 0], i, depth).astype(F32)
        add_taps(taps_ref, i, suffix, [wide_ref[i, j].astype(F32) for j in range(CW)])
    weights = (scale * (near_ref[...] + taps_ref[...])).astype(BF16)
    for n in range(weights_ref.shape[0]):
        weights_ref[n] = weights
    place = out_ref.at[:, pl.ds(size, CW * HALF)]
    weights = pltpu.make_async_copy(weights_ref, place, sems.at[1])
    weights.start()
    done_ref[...] = jnp.zeros(done_ref.shape, F32)
    states.wait()
    weights.wait()


def query_side_kernel(
    core_ref,
    chip_ref,
    k_ref,
    g_ref,
    head_ref,
    edge_ref,
    w_ref,
    done_ref,
    c_ref,
    gc_ref,
    q_ref,
    gk_ref,
    gv_ref,
    send_ref,
    gq_ref,
    own_ref,
    hold_ref,
    sems,
    fetch_sems,
    *,
    scale,
):
    core = core_ref[0]
    rows = k_ref.shape[0]
    depth = chip_ref.shape[2]
    seen = later(rows)
    fetches = [
        pltpu.make_async_copy(ref, hold_ref.at[n], fetch_sems.at[n])
        for n, ref in enumerate((c_ref, q_ref, gc_ref))
    ]
    for fetch in fetches:
        fetch.start()
    for fetch in fetches:
        fetch.wait()
    for i in range(HALF):
        at = columns(i)
        suffix = head_state(lambda n: chip_ref[n, 0], i, depth)
        c = jnp.concatenate([head_ref[:, at], hold_ref[0, HALO:, at]], axis=0)
        g, k = g_ref[:, at], k_ref[:, at]
        attn = jnp.where(seen.T, dot(g, c, (1, 1)), 0.0)
        gq_ref[:, at] = dot(attn.astype(BF16), k, (1, 0)).astype(BF16)
        turned = jnp.where(seen, dot(c, g, (1, 1)), 0.0)
        gk = dot(turned.astype(BF16), hold_ref[1, :, at], (1, 0))
        gk = scale * (gk + dot(c, suffix, (1, 1)))
        gc = scale * (hold_ref[2, :, at].astype(F32) + dot(k, suffix, (1, 0)))
        edge = edge_ref[...].astype(F32)[2 * EDGE * i : 2 * EDGE * (i + 1)]
        after = edge[:EDGE] + dot(edge.astype(BF16), suffix, (1, 0))[EDGE:]
        ext = jnp.concatenate([gc, scale * after, jnp.zeros((TILE - EDGE, DH), F32)], axis=0)
        taps = tap_rows(w_ref, core, i)
        gv = taps[0:1] * gc
        for j in range(1, CW):
            gv = gv + taps[j : j + 1] * ext[j : j + rows]
        for n, value in enumerate((gk, gv)):
            low, high = value[: rows // 2].astype(BF16), value[rows // 2 :].astype(BF16)
            own_ref[n, :, at] = jnp.where(core == 0, low, high)
            send_ref[n, :, at] = jnp.where(core == 0, high, low)
    put(own_ref, core, (gk_ref, gv_ref), sems)


def put(half_ref, side, refs, sems):
    copies = [
        pltpu.make_async_copy(half_ref.at[n], ref.at[:, half_of(side, WIDE)], sems.at[n])
        for n, ref in enumerate(refs)
    ]
    for copy in copies:
        copy.start()
    for copy in copies:
        copy.wait()


def key_side_kernel(
    core_ref, chip_ref, g_ref, gq_ref, own_ref, send_ref, taps_ref, *, scale, depth, slots
):
    core = core_ref[0]
    rows = g_ref.shape[0]
    chips, size, _ = chip_ref.shape
    for i in range(HALF):
        at = columns(i)
        prefix = head_state(lambda n: chip_ref[slots[n], :depth], i, depth)
        gq = scale * (gq_ref[:, at].astype(F32) + dot(g_ref[:, at], prefix, (1, 1)))
        low, high = gq[: rows // 2].astype(BF16), gq[rows // 2 :].astype(BF16)
        own_ref[:, at] = jnp.where(core == 0, low, high)
        send_ref[:, at] = jnp.where(core == 0, high, low)
    total = chip_ref[0, size - CW * HALF :].astype(F32)
    for n in range(1, chips):
        total = total + chip_ref[n, size - CW * HALF :].astype(F32)
    taps_ref[...] = total


def join_kernel(core_ref, recv_ref, _, __, gk_ref, gv_ref, sems):
    put(recv_ref, 1 - core_ref[0], (gk_ref, gv_ref), sems)


def finish_kernel(
    core_ref, own_ref, recv_ref, taps_ref, far_ref, gq_ref, gw_ref, hold_ref, sems
):
    core = core_ref[0]
    copies = [
        pltpu.make_async_copy(ref, gq_ref.at[:, half_of(side, WIDE)], sems.at[n])
        for n, (side, ref) in enumerate(((1 - core, recv_ref), (core, own_ref)))
    ]
    for copy in copies:
        copy.start()
    for side, ref in ((core, taps_ref), (1 - core, far_ref)):
        for i in range(HALF):
            at = pl.ds(pl.multiple_of(side * WIDE + i * DH, DH), DH)
            for j in range(CW):
                row = j * HALF + i
                hold_ref[j : j + 1, at] = ref[row : row + 1, :]
    copies.append(pltpu.make_async_copy(hold_ref, gw_ref, sems.at[2]))
    copies[-1].start()
    for copy in copies:
        copy.wait()


def local(queries, keys, values, grad_out, conv_weight):
    rows, width = queries.shape
    lines, line = lax.axis_size("row"), lax.axis_size("col") // 2
    count = 2 * lines * line
    chips = lines * line
    depth = WIDE // chips
    scale = (DH * rows * count) ** (-0.5)
    core = lax.rem(lax.axis_index("col"), 2).astype(jnp.int32).reshape(1)
    half = line // 2
    along = [z for n in range(half) for z in (half + n, n)]
    listed = [r * line + z for r in reversed(range(lines)) for z in along]
    groups = [[2 * p + c for p in listed] for c in range(2)]
    order = tuple(listed.index(p) for p in range(chips))
    final = listed
    final_groups = [[2 * p + c for p in final] for c in range(2)]
    places = tuple((order[p], final.index(p)) for p in range(chips))
    slots = tuple(final.index(p) for p in listed)

    def swap(value):
        return lax.ppermute(value, AXES, [(d, d ^ 1) for d in range(count)])

    def shifted(value, by):
        pairs = [(d, d + by) for d in range(count) if 0 <= d + by < count]
        return lax.ppermute(value, AXES, pairs)

    def turn(value, groups):
        return lax.all_to_all(value, AXES, 0, 0, axis_index_groups=groups, tiled=True)

    pair = shape((2, rows, WIDE))
    block = shape((2 * rows, WIDE))
    far_block = pltpu.HBM((2 * rows, WIDE), BF16)
    states = shape((HALF, DH, DH))
    edges = shape((HALO, WIDE))
    flag = shape((8, DH), F32)
    dma = pltpu.SemaphoreType.DMA
    padded = max(depth, HALO)

    def in_hbm(value):
        return pltpu.with_memory_space_constraint(value, pltpu.HBM)

    queries, grad_out, keys, values = map(in_hbm, (queries, grad_out, keys, values))
    q_keep, q_give = call(
        query_state_kernel,
        (states, states),
        core,
        [queries, grad_out],
        [pltpu.VMEM((2, rows, width), BF16), dma((2,))],
        [ANY] * 2,
    )
    q_recv = swap(q_give)
    longer = shape((2, rows + HALO, WIDE))
    kv_own, kv_send = call(
        split_key_kernel,
        (longer, longer),
        core,
        [keys, values, queries, grad_out, q_keep],
        [dma((2, 2, 2))],
        [ANY] * 4 + [VMEM],
    )
    kv_recv = swap(kv_send)
    q_sent, added = call(
        add_kernel,
        (states, flag),
        core,
        [q_keep, q_recv],
    )
    q_turned = turn(q_sent.reshape(chips, depth, DH), groups)
    qg_own, qg_send = call(
        split_kernel,
        (pair, pair),
        core,
        [queries, grad_out, added],
        [dma((2, 2))],
        [ANY, ANY, VMEM],
    )
    qg_recv = swap(qg_send)
    k, v, tail, edge = call(
        gather_key_kernel,
        (block, block, shape((EDGE * HALF, DH)), shape((2 * EDGE * HALF, DH))),
        core,
        [kv_own, kv_recv],
    )
    halo = shifted(tail, 2)
    q, g, q_far = call(
        gather_query_kernel,
        (block, block, far_block),
        core,
        [qg_own, qg_recv],
        [dma(())],
        made=(VMEM, VMEM, ANY),
    )
    c, k_state = call(
        conv_kernel,
        (far_block, shape((HALF, DH, DH), F32)),
        core,
        [k, v, conv_weight],
    )
    both, c_head, turned = call(
        functools.partial(turn_kernel, order=order),
        (shape((chips, 2, depth, DH)), edges, flag),
        core,
        [q_turned, k_state, k, v, halo, conv_weight],
    )
    both = turn(both, groups)
    gc, taps, wide = call(
        score_kernel,
        (far_block, shape((CW * HALF, DH), F32), shape((HALF, CW, DH, DH))),
        core,
        [q, g, k, v, halo]
    )
    edge = shifted(edge, -2)
    last, tapped = call(
        functools.partial(tap_kernel, scale=scale, places=places),
        (pltpu.HBM((chips, padded + CW * HALF, DH), BF16), flag),
        core,
        [both, wide, taps, edge],
        [
            pltpu.VMEM((CW * HALF, DH), F32),
            pltpu.VMEM((chips, padded, DH), BF16),
            pltpu.VMEM((chips, CW * HALF, DH), BF16),
            dma((2,)),
        ],
        made=(ANY, VMEM),
    )
    last = turn(last, final_groups)
    full = shape((rows, width))
    grad_keys, grad_values, kv_give, gq = call(
        functools.partial(query_side_kernel, scale=scale),
        (full, full, pair, block),
        core,
        [both, k, g, c_head, edge, conv_weight, tapped, *map(in_hbm, (c, gc, q_far))],
        [pltpu.VMEM((2, rows, WIDE), BF16), pltpu.VMEM((3, 2 * rows, WIDE), BF16)]
        + [dma((2,)), dma((3,))],
        [VMEM] * 7 + [ANY] * 3,
        (ANY, ANY, VMEM, VMEM),
    )
    kv_got = swap(kv_give)
    q_grad, q_give, taps = call(
        functools.partial(key_side_kernel, scale=scale, depth=depth, slots=slots),
        (shape((rows, WIDE)), shape((rows, WIDE)), shape((CW * HALF, DH), F32)),
        core,
        [last, g, gq],
    )
    q_got = swap(q_give)
    far = swap(taps)
    grad_keys, grad_values = call(
        join_kernel,
        (full, full),
        core,
        [kv_got, grad_keys, grad_values],
        [dma((2,))],
        [VMEM, ANY, ANY],
        (ANY, ANY),
        {2: 0, 3: 1},
    )
    grad_queries, grad_weight = call(
        finish_kernel,
        (full, shape((CW, width), F32)),
        core,
        [q_grad, q_got, taps, far],
        [pltpu.VMEM((CW, width), F32), dma((3,))],
        made=(ANY, ANY),
    )
    return grad_queries, grad_keys, grad_values, grad_weight


def solution(mesh):
    placed = (
        P(("row", "col"), None),
        P(("row", "col"), None),
        P(("row", "col"), None),
        P(("row", "col"), None),
        P(),
    )
    return jax.shard_map(
        local,
        mesh=mesh,
        in_specs=placed,
        out_specs=(P(("row", "col"), None), P(("row", "col"), None), P(("row", "col"), None), P()),
        check_vma=False,
    )
```

```python
import functools

import jax
import jax.numpy as jnp
from jax import lax
from jax.experimental import pallas as pl
from jax.experimental.pallas import tpu as pltpu
from jax.sharding import PartitionSpec as P

HEADS = 16
DH = 128
CW = 4
HALF = HEADS // 2
WIDE = HALF * DH
EDGE = 4
TILE = 8
HALO = 16
AXES = ("row", "col")
F32 = jnp.float32
BF16 = jnp.bfloat16
VMEM = pl.BlockSpec(memory_space=pltpu.VMEM)
SMEM = pl.BlockSpec(memory_space=pltpu.SMEM)
ANY = pl.BlockSpec(memory_space=pl.ANY)
PARAMS = pltpu.CompilerParams(vmem_limit_bytes=16 * 1024 * 1024)


def dot(a, b, over):
    return lax.dot_general(a, b, ((over[:1], over[1:]), ((), ())), preferred_element_type=F32)


def columns(head):
    return pl.ds(head * DH, DH)


def half_of(core, size):
    return pl.ds(pl.multiple_of(core * size, size), size)


def call(kernel, outs, core, arrays, scratch=(), given=None, made=None, aliases={}):
    return pl.pallas_call(
        kernel,
        out_shape=outs,
        in_specs=[SMEM] + (given or [VMEM] * len(arrays)),
        out_specs=made or jax.tree.map(lambda _: VMEM, outs),
        scratch_shapes=scratch,
        input_output_aliases=aliases,
        compiler_params=PARAMS,
    )(core, *arrays)


def shape(dims, dtype=BF16):
    return jax.ShapeDtypeStruct(dims, dtype)


def split_key_kernel(
    core_ref, k_ref, v_ref, q_ref, g_ref, after_ref, own_ref, send_ref, sems
):
    core = core_ref[0]
    rows = k_ref.shape[0]
    copies = []
    for n, refs in enumerate(((k_ref, q_ref), (v_ref, g_ref))):
        for m, (out, side) in enumerate(((send_ref, 1 - core), (own_ref, core))):
            for e, (ref, first, size) in enumerate(zip(refs, (0, rows), (rows, HALO))):
                part = ref.at[pl.ds(0, size), half_of(side, WIDE)]
                place = out.at[n, pl.ds(first, size)]
                copies.append(pltpu.make_async_copy(part, place, sems.at[n, m, e]))
    for copy in copies:
        copy.start()
    for copy in copies:
        copy.wait()


def split_kernel(core_ref, a_ref, b_ref, after_ref, own_ref, send_ref, sems):
    core = core_ref[0]
    copies = []
    for n, ref in enumerate((a_ref, b_ref)):
        for m, (out, side) in enumerate(((send_ref, 1 - core), (own_ref, core))):
            copies.append(
                pltpu.make_async_copy(ref.at[:, half_of(side, WIDE)], out.at[n], sems.at[n, m])
            )
    for copy in copies:
        copy.start()
    for copy in copies:
        copy.wait()


def query_state_kernel(
    core_ref, q_ref, g_ref, keep_ref, give_ref, held_ref, sems
):
    core = core_ref[0]
    copies = [
        pltpu.make_async_copy(ref, held_ref.at[n], sems.at[n])
        for n, ref in enumerate((q_ref, g_ref))
    ]
    for copy in copies:
        copy.start()
    for copy in copies:
        copy.wait()
    for side, out in ((1 - core, give_ref), (core, keep_ref)):
        for i in range(HALF):
            at = pl.ds(pl.multiple_of(side * WIDE + i * DH, DH), DH)
            out[i] = dot(held_ref[0, :, at], held_ref[1, :, at], (0, 0)).astype(BF16)


def add_kernel(core_ref, keep_ref, recv_ref, out_ref, done_ref):
    for i in range(HALF):
        out_ref[i] = (keep_ref[i].astype(F32) + recv_ref[i].astype(F32)).astype(BF16)
    done_ref[...] = jnp.zeros(done_ref.shape, F32)


def gather(core, own_ref, recv_ref, refs):
    for n, ref in enumerate(refs):
        rows = ref.shape[0] // 2
        ref[half_of(core, rows), :] = own_ref[n, :rows]
        ref[half_of(1 - core, rows), :] = recv_ref[n, :rows]


def gather_query_kernel(core_ref, own_ref, recv_ref, q_ref, g_ref, far_ref, sem):
    gather(core_ref[0], own_ref, recv_ref, (q_ref, g_ref))
    copy = pltpu.make_async_copy(q_ref, far_ref, sem)
    copy.start()
    copy.wait()


def tail_kernel(core_ref, own_ref, recv_ref, tail_ref):
    rows = own_ref.shape[1] - HALO
    tails = []
    for i in range(HALF):
        at = columns(i)
        own, recv = (ref[1, rows - HALO : rows, at] for ref in (own_ref, recv_ref))
        tail = jnp.where(core_ref[0] == 1, own, recv)
        tails.append(tail.astype(F32)[HALO - EDGE :])
    tail_ref[...] = jnp.concatenate(tails, axis=0).astype(BF16)


def gather_key_kernel(core_ref, own_ref, recv_ref, k_ref, v_ref, edge_ref):
    core = core_ref[0]
    gather(core, own_ref, recv_ref, (k_ref, v_ref))
    rows = k_ref.shape[0]
    edges = []
    first = lax.broadcasted_iota(jnp.int32, (HALO, HALO), 0)
    unseen = first > lax.broadcasted_iota(jnp.int32, (HALO, HALO), 1)
    for i in range(HALF):
        at = columns(i)
        q, g = (
            jnp.where(core == 0, own_ref[n, rows // 2 :, at], recv_ref[n, rows // 2 :, at])
            for n in range(2)
        )
        k = k_ref[:HALO, at]
        score = jnp.where(unseen, dot(k, q, (1, 1)), 0.0).astype(BF16)
        edges += [-dot(score, g, (1, 0))[:EDGE], k.astype(F32)[:EDGE]]
    edge_ref[...] = jnp.concatenate(edges, axis=0).astype(BF16)


def lagged(v, halo_ref, head):
    halo = halo_ref[...].astype(F32)[head * EDGE : (head + 1) * EDGE]
    ext = jnp.concatenate([jnp.zeros((TILE - EDGE, DH), F32), halo, v.astype(F32)], axis=0)
    return [ext[TILE - j : TILE - j + v.shape[0]] for j in range(CW)]


def tap_rows(w_ref, core, head):
    return w_ref[:, pl.ds(pl.multiple_of(core * WIDE + head * DH, DH), DH)]


def later(rows):
    first = lax.broadcasted_iota(jnp.int32, (rows, rows), 0)
    return first <= lax.broadcasted_iota(jnp.int32, (rows, rows), 1)


def tap_states(wide_ref, head, k, parts):
    for j, part in enumerate(parts):
        wide_ref[head, j] = dot(k, part.astype(BF16), (0, 0)).astype(BF16)


def add_taps(taps_ref, head, grad, parts):
    for j, part in enumerate(parts):
        row = j * HALF + head
        taps_ref[row : row + 1, :] = jnp.sum(grad * part, axis=0, keepdims=True)


def score_kernel(
    core_ref, q_ref, g_ref, k_ref, v_ref, halo_ref, gc_ref, taps_ref, wide_ref
):
    seen = later(q_ref.shape[0])
    for i in range(HALF):
        at = columns(i)
        k = k_ref[:, at]
        score = jnp.where(seen, dot(k, q_ref[:, at], (1, 1)), 0.0).astype(BF16)
        gc = dot(score, g_ref[:, at], (1, 0))
        gc_ref[:, at] = gc.astype(BF16)
        parts = lagged(v_ref[:, at], halo_ref, i)
        add_taps(taps_ref, i, gc, parts)
        tap_states(wide_ref, i, k, parts)


def convolved(w_ref, core, head, parts):
    taps = tap_rows(w_ref, core, head)
    acc = taps[0:1] * parts[0]
    for j in range(1, CW):
        acc = acc + taps[j : j + 1] * parts[j]
    return acc


def conv_kernel(core_ref, k_ref, v_ref, w_ref, c_ref, state_ref):
    rows = v_ref.shape[0]
    body = lax.broadcasted_iota(jnp.int32, (rows, DH), 0) >= HALO
    for i in range(HALF):
        at = columns(i)
        v = v_ref[:, at].astype(F32)
        ext = jnp.concatenate([jnp.zeros((HALO, DH), F32), v], axis=0)
        parts = [ext[HALO - j : HALO - j + rows] for j in range(CW)]
        c = jnp.where(body, convolved(w_ref, core_ref[0], i, parts), 0.0).astype(BF16)
        c_ref[:, at] = c
        state_ref[i] = dot(k_ref[:, at], c, (0, 0))


def turn_kernel(
    core_ref,
    q_ref,
    state_ref,
    k_ref,
    v_ref,
    halo_ref,
    w_ref,
    out_ref,
    head_ref,
    done_ref,
    *,
    turns,
):
    depth = q_ref.shape[1]
    for i in range(HALF):
        at = columns(i)
        parts = lagged(v_ref[:HALO, at], halo_ref, i)
        c = convolved(w_ref, core_ref[0], i, parts).astype(BF16)
        head_ref[:, at] = c
        state = state_ref[i] + dot(k_ref[:HALO, at], c, (0, 0))
        for n in range(DH // depth):
            part = state[n * depth : (n + 1) * depth].astype(BF16)
            out_ref[i * (DH // depth) + n, 1] = part
    total = jnp.zeros(q_ref.shape[1:], F32)
    for n, slot in reversed(turns):
        out_ref[slot, 0] = total.astype(BF16)
        total = total + q_ref[n].astype(F32)
    done_ref[...] = jnp.zeros(done_ref.shape, F32)


def head_state(read, head, depth):
    parts = DH // depth
    if depth % HALO == 0:
        return jnp.concatenate([read(head * parts + n) for n in range(parts)], axis=0)
    found = [read(head * parts + n).astype(F32) for n in range(parts)]
    return jnp.concatenate(found, axis=0).astype(BF16)


def tap_kernel(
    core_ref,
    chip_ref,
    wide_ref,
    near_ref,
    edge_ref,
    out_ref,
    done_ref,
    taps_ref,
    *,
    scale,
    places,
    ways,
):
    depth = chip_ref.shape[2]
    size = out_ref.shape[1] - CW * HALF
    total = jnp.zeros((depth, DH), F32)
    for n, slot in places:
        out_ref[slot, :depth] = total.astype(BF16)
        if depth < size:
            out_ref[slot, depth:size] = jnp.zeros((size - depth, DH), BF16)
        total = total + chip_ref[n, 1].astype(F32)
    for i in range(HALF):
        suffix = head_state(lambda n: chip_ref[ways[n], 0], i, depth).astype(F32)
        add_taps(taps_ref, i, suffix, [wide_ref[i, j].astype(F32) for j in range(CW)])
    weights = (scale * (near_ref[...] + taps_ref[...])).astype(BF16)
    for n in range(out_ref.shape[0]):
        out_ref[n, size:] = weights
    done_ref[...] = jnp.zeros(done_ref.shape, F32)


def query_side_kernel(
    core_ref,
    chip_ref,
    k_ref,
    g_ref,
    head_ref,
    edge_ref,
    w_ref,
    done_ref,
    c_ref,
    gc_ref,
    q_ref,
    gk_ref,
    gv_ref,
    send_ref,
    gq_ref,
    own_ref,
    hold_ref,
    sems,
    fetch_sems,
    *,
    scale,
    ways,
):
    core = core_ref[0]
    rows = k_ref.shape[0]
    depth = chip_ref.shape[2]
    seen = later(rows)
    fetches = [
        pltpu.make_async_copy(ref, hold_ref.at[n], fetch_sems.at[n])
        for n, ref in enumerate((c_ref, q_ref, gc_ref))
    ]
    for fetch in fetches:
        fetch.start()
    for fetch in fetches:
        fetch.wait()
    for i in range(HALF):
        at = columns(i)
        suffix = head_state(lambda n: chip_ref[ways[n], 0], i, depth)
        c = jnp.concatenate([head_ref[:, at], hold_ref[0, HALO:, at]], axis=0)
        g, k = g_ref[:, at], k_ref[:, at]
        attn = jnp.where(seen.T, dot(g, c, (1, 1)), 0.0)
        gq_ref[:, at] = dot(attn.astype(BF16), k, (1, 0)).astype(BF16)
        turned = jnp.where(seen, dot(c, g, (1, 1)), 0.0)
        gk = dot(turned.astype(BF16), hold_ref[1, :, at], (1, 0))
        gk = scale * (gk + dot(c, suffix, (1, 1)))
        gc = scale * (hold_ref[2, :, at].astype(F32) + dot(k, suffix, (1, 0)))
        edge = edge_ref[...].astype(F32)[2 * EDGE * i : 2 * EDGE * (i + 1)]
        after = edge[:EDGE] + dot(edge.astype(BF16), suffix, (1, 0))[EDGE:]
        ext = jnp.concatenate([gc, scale * after, jnp.zeros((TILE - EDGE, DH), F32)], axis=0)
        taps = tap_rows(w_ref, core, i)
        gv = taps[0:1] * gc
        for j in range(1, CW):
            gv = gv + taps[j : j + 1] * ext[j : j + rows]
        for n, value in enumerate((gk, gv)):
            low, high = value[: rows // 2].astype(BF16), value[rows // 2 :].astype(BF16)
            own_ref[n, :, at] = jnp.where(core == 0, low, high)
            send_ref[n, :, at] = jnp.where(core == 0, high, low)
    put(own_ref, core, (gk_ref, gv_ref), sems)


def put(half_ref, side, refs, sems):
    copies = [
        pltpu.make_async_copy(half_ref.at[n], ref.at[:, half_of(side, WIDE)], sems.at[n])
        for n, ref in enumerate(refs)
    ]
    for copy in copies:
        copy.start()
    for copy in copies:
        copy.wait()


def key_side_kernel(
    core_ref, chip_ref, g_ref, gq_ref, own_ref, send_ref, taps_ref, *, scale, depth, slots
):
    core = core_ref[0]
    rows = g_ref.shape[0]
    chips, size, _ = chip_ref.shape
    for i in range(HALF):
        at = columns(i)
        prefix = head_state(lambda n: chip_ref[slots[n], :depth], i, depth)
        gq = scale * (gq_ref[:, at].astype(F32) + dot(g_ref[:, at], prefix, (1, 1)))
        low, high = gq[: rows // 2].astype(BF16), gq[rows // 2 :].astype(BF16)
        own_ref[:, at] = jnp.where(core == 0, low, high)
        send_ref[:, at] = jnp.where(core == 0, high, low)
    total = chip_ref[0, size - CW * HALF :].astype(F32)
    for n in range(1, chips):
        total = total + chip_ref[n, size - CW * HALF :].astype(F32)
    taps_ref[...] = total


def join_kernel(core_ref, recv_ref, own_ref, _, __, gk_ref, gv_ref, gq_ref, sems, sem):
    core = core_ref[0]
    copy = pltpu.make_async_copy(own_ref, gq_ref.at[:, half_of(core, WIDE)], sem)
    copy.start()
    put(recv_ref, 1 - core, (gk_ref, gv_ref), sems)
    copy.wait()


def finish_kernel(
    core_ref, recv_ref, taps_ref, far_ref, _, gq_ref, gw_ref, hold_ref, sems
):
    core = core_ref[0]
    place = gq_ref.at[:, half_of(1 - core, WIDE)]
    copies = [pltpu.make_async_copy(recv_ref, place, sems.at[0])]
    copies[0].start()
    for side, ref in ((core, taps_ref), (1 - core, far_ref)):
        for i in range(HALF):
            at = pl.ds(pl.multiple_of(side * WIDE + i * DH, DH), DH)
            for j in range(CW):
                row = j * HALF + i
                hold_ref[j : j + 1, at] = ref[row : row + 1, :]
    copies.append(pltpu.make_async_copy(hold_ref, gw_ref, sems.at[1]))
    copies[1].start()
    for copy in copies:
        copy.wait()


def local(queries, keys, values, grad_out, conv_weight):
    rows, width = queries.shape
    lines, line = lax.axis_size("row"), lax.axis_size("col") // 2
    count = 2 * lines * line
    chips = lines * line
    depth = WIDE // chips
    scale = (DH * rows * count) ** (-0.5)
    core = lax.rem(lax.axis_index("col"), 2).astype(jnp.int32).reshape(1)
    half = line // 2
    split = [*reversed(range(half)), *range(half, line)]
    mixed = [z for n in range(half) for z in (half + n, n)]
    lists = [
        [r * line + z for r in reversed(range(lines)) for z in along]
        for along in (split, mixed, mixed)
    ]
    groups = [[[2 * p + c for p in each] for c in range(2)] for each in lists]
    spots = [[each.index(p) for p in range(chips)] for each in lists]
    turns = tuple(zip(spots[0], spots[1]))
    places = tuple(zip(spots[1], spots[2]))
    ways = tuple(spots[1][p] for p in lists[0])
    slots = tuple(spots[2][p] for p in lists[1])

    def swap(value):
        return lax.ppermute(value, AXES, [(d, d ^ 1) for d in range(count)])

    def shifted(value, by):
        pairs = [(d, d + by) for d in range(count) if 0 <= d + by < count]
        return lax.ppermute(value, AXES, pairs)

    def turn(value, groups):
        return lax.all_to_all(value, AXES, 0, 0, axis_index_groups=groups, tiled=True)

    pair = shape((2, rows, WIDE))
    block = shape((2 * rows, WIDE))
    far_block = pltpu.HBM((2 * rows, WIDE), BF16)
    states = shape((HALF, DH, DH))
    edges = shape((HALO, WIDE))
    flag = shape((8, DH), F32)
    dma = pltpu.SemaphoreType.DMA
    padded = max(depth, HALO)

    def in_hbm(value):
        return pltpu.with_memory_space_constraint(value, pltpu.HBM)

    queries, grad_out, keys, values = map(in_hbm, (queries, grad_out, keys, values))
    q_keep, q_give = call(
        query_state_kernel,
        (states, states),
        core,
        [queries, grad_out],
        [pltpu.VMEM((2, rows, width), BF16), dma((2,))],
        [ANY] * 2,
    )
    q_recv = swap(q_give)
    longer = shape((2, rows + HALO, WIDE))
    kv_own, kv_send = call(
        split_key_kernel,
        (longer, longer),
        core,
        [keys, values, queries, grad_out, q_keep],
        [dma((2, 2, 2))],
        [ANY] * 4 + [VMEM],
    )
    kv_recv = swap(kv_send)
    q_sent, added = call(
        add_kernel,
        (states, flag),
        core,
        [q_keep, q_recv],
    )
    q_turned = turn(q_sent.reshape(chips, depth, DH), groups[0])
    qg_own, qg_send = call(
        split_kernel,
        (pair, pair),
        core,
        [queries, grad_out, added],
        [dma((2, 2))],
        [ANY, ANY, VMEM],
    )
    qg_recv = swap(qg_send)
    tail = call(tail_kernel, shape((EDGE * HALF, DH)), core, [kv_own, kv_recv])
    k, v, edge = call(
        gather_key_kernel,
        (block, block, shape((2 * EDGE * HALF, DH))),
        core,
        [kv_own, kv_recv],
    )
    halo = shifted(tail, 2)
    q, g, q_far = call(
        gather_query_kernel,
        (block, block, far_block),
        core,
        [qg_own, qg_recv],
        [dma(())],
        made=(VMEM, VMEM, ANY),
    )
    c, k_state = call(
        conv_kernel,
        (far_block, shape((HALF, DH, DH), F32)),
        core,
        [k, v, conv_weight],
    )
    both, c_head, turned = call(
        functools.partial(turn_kernel, turns=turns),
        (shape((chips, 2, depth, DH)), edges, flag),
        core,
        [q_turned, k_state, k, v, halo, conv_weight],
    )
    both = turn(both, groups[1])
    gc, taps, wide = call(
        score_kernel,
        (far_block, shape((CW * HALF, DH), F32), shape((HALF, CW, DH, DH))),
        core,
        [q, g, k, v, halo]
    )
    edge = shifted(edge, -2)
    last, tapped = call(
        functools.partial(tap_kernel, scale=scale, places=places, ways=ways),
        (shape((chips, padded + CW * HALF, DH)), flag),
        core,
        [both, wide, taps, edge],
        [pltpu.VMEM((CW * HALF, DH), F32)],
    )
    last = turn(last, groups[2])
    full = shape((rows, width))
    grad_keys, grad_values, kv_give, gq = call(
        functools.partial(query_side_kernel, scale=scale, ways=ways),
        (full, full, pair, block),
        core,
        [both, k, g, c_head, edge, conv_weight, tapped, *map(in_hbm, (c, gc, q_far))],
        [pltpu.VMEM((2, rows, WIDE), BF16), pltpu.VMEM((3, 2 * rows, WIDE), BF16)]
        + [dma((2,)), dma((3,))],
        [VMEM] * 7 + [ANY] * 3,
        (ANY, ANY, VMEM, VMEM),
    )
    kv_got = swap(kv_give)
    q_grad, q_give, taps = call(
        functools.partial(key_side_kernel, scale=scale, depth=depth, slots=slots),
        (shape((rows, WIDE)), shape((rows, WIDE)), shape((CW * HALF, DH), F32)),
        core,
        [last, g, gq],
    )
    q_got = swap(q_give)
    far = swap(taps)
    grad_keys, grad_values, grad_queries = call(
        join_kernel,
        (full, full, full),
        core,
        [kv_got, q_grad, grad_keys, grad_values],
        [dma((2,)), dma(())],
        [VMEM, VMEM, ANY, ANY],
        (ANY, ANY, ANY),
        {3: 0, 4: 1},
    )
    grad_queries, grad_weight = call(
        finish_kernel,
        (full, shape((CW, width), F32)),
        core,
        [q_got, taps, far, grad_queries],
        [pltpu.VMEM((CW, width), F32), dma((2,))],
        [VMEM, VMEM, VMEM, ANY],
        (ANY, ANY),
        {4: 0},
    )
    return grad_queries, grad_keys, grad_values, grad_weight


def solution(mesh):
    placed = (
        P(("row", "col"), None),
        P(("row", "col"), None),
        P(("row", "col"), None),
        P(("row", "col"), None),
        P(),
    )
    return jax.shard_map(
        local,
        mesh=mesh,
        in_specs=placed,
        out_specs=(P(("row", "col"), None), P(("row", "col"), None), P(("row", "col"), None), P()),
        check_vma=False,
    )
```

```python
import functools

import jax
import jax.numpy as jnp
from jax import lax
from jax.experimental import pallas as pl
from jax.experimental.pallas import tpu as pltpu
from jax.sharding import PartitionSpec as P

HEADS = 16
DH = 128
CW = 4
HALF = HEADS // 2
WIDE = HALF * DH
EDGE = 4
TILE = 8
HALO = 16
AXES = ("row", "col")
F32 = jnp.float32
BF16 = jnp.bfloat16
VMEM = pl.BlockSpec(memory_space=pltpu.VMEM)
SMEM = pl.BlockSpec(memory_space=pltpu.SMEM)
ANY = pl.BlockSpec(memory_space=pl.ANY)
PARAMS = pltpu.CompilerParams(vmem_limit_bytes=16 * 1024 * 1024)


def dot(a, b, over):
    return lax.dot_general(a, b, ((over[:1], over[1:]), ((), ())), preferred_element_type=F32)


def columns(head):
    return pl.ds(head * DH, DH)


def half_of(core, size):
    return pl.ds(pl.multiple_of(core * size, size), size)


def call(kernel, outs, core, arrays, scratch=(), given=None, made=None, aliases={}):
    return pl.pallas_call(
        kernel,
        out_shape=outs,
        in_specs=[SMEM] + (given or [VMEM] * len(arrays)),
        out_specs=made or jax.tree.map(lambda _: VMEM, outs),
        scratch_shapes=scratch,
        input_output_aliases=aliases,
        compiler_params=PARAMS,
    )(core, *arrays)


def shape(dims, dtype=BF16):
    return jax.ShapeDtypeStruct(dims, dtype)


def split_key_kernel(
    core_ref, k_ref, v_ref, q_ref, g_ref, after_ref, own_ref, send_ref, sems
):
    core = core_ref[0]
    rows = k_ref.shape[0]
    copies = []
    for n, refs in enumerate(((k_ref, q_ref), (v_ref, g_ref))):
        for m, (out, side) in enumerate(((send_ref, 1 - core), (own_ref, core))):
            for e, (ref, first, size) in enumerate(zip(refs, (0, rows), (rows, HALO))):
                part = ref.at[pl.ds(0, size), half_of(side, WIDE)]
                place = out.at[n, pl.ds(first, size)]
                copies.append(pltpu.make_async_copy(part, place, sems.at[n, m, e]))
    for copy in copies:
        copy.start()
    for copy in copies:
        copy.wait()


def split_kernel(core_ref, a_ref, b_ref, after_ref, own_ref, send_ref, sems):
    core = core_ref[0]
    copies = []
    for n, ref in enumerate((a_ref, b_ref)):
        for m, (out, side) in enumerate(((send_ref, 1 - core), (own_ref, core))):
            copies.append(
                pltpu.make_async_copy(ref.at[:, half_of(side, WIDE)], out.at[n], sems.at[n, m])
            )
    for copy in copies:
        copy.start()
    for copy in copies:
        copy.wait()


def query_state_kernel(
    core_ref, q_ref, g_ref, keep_ref, give_ref, held_ref, sems
):
    core = core_ref[0]
    copies = [
        pltpu.make_async_copy(ref, held_ref.at[n], sems.at[n])
        for n, ref in enumerate((q_ref, g_ref))
    ]
    for copy in copies:
        copy.start()
    for copy in copies:
        copy.wait()
    for side, out in ((1 - core, give_ref), (core, keep_ref)):
        for i in range(HALF):
            at = pl.ds(pl.multiple_of(side * WIDE + i * DH, DH), DH)
            out[i] = dot(held_ref[0, :, at], held_ref[1, :, at], (0, 0)).astype(BF16)


def add_kernel(core_ref, keep_ref, recv_ref, out_ref, done_ref):
    for i in range(HALF):
        out_ref[i] = (keep_ref[i].astype(F32) + recv_ref[i].astype(F32)).astype(BF16)
    done_ref[...] = jnp.zeros(done_ref.shape, F32)


def gather(core, own_ref, recv_ref, refs):
    for n, ref in enumerate(refs):
        rows = ref.shape[0] // 2
        ref[half_of(core, rows), :] = own_ref[n, :rows]
        ref[half_of(1 - core, rows), :] = recv_ref[n, :rows]


def gather_query_kernel(core_ref, own_ref, recv_ref, q_ref, g_ref, far_ref, sem):
    gather(core_ref[0], own_ref, recv_ref, (q_ref, g_ref))
    copy = pltpu.make_async_copy(q_ref, far_ref, sem)
    copy.start()
    copy.wait()


def tail_kernel(core_ref, own_ref, recv_ref, tail_ref):
    rows = own_ref.shape[1] - HALO
    tails = []
    for i in range(HALF):
        at = columns(i)
        own, recv = (ref[1, rows - HALO : rows, at] for ref in (own_ref, recv_ref))
        tail = jnp.where(core_ref[0] == 1, own, recv)
        tails.append(tail.astype(F32)[HALO - EDGE :])
    tail_ref[...] = jnp.concatenate(tails, axis=0).astype(BF16)


def gather_key_kernel(core_ref, own_ref, recv_ref, k_ref, v_ref, edge_ref):
    core = core_ref[0]
    gather(core, own_ref, recv_ref, (k_ref, v_ref))
    rows = k_ref.shape[0]
    edges = []
    first = lax.broadcasted_iota(jnp.int32, (HALO, HALO), 0)
    unseen = first > lax.broadcasted_iota(jnp.int32, (HALO, HALO), 1)
    for i in range(HALF):
        at = columns(i)
        q, g = (
            jnp.where(core == 0, own_ref[n, rows // 2 :, at], recv_ref[n, rows // 2 :, at])
            for n in range(2)
        )
        k = k_ref[:HALO, at]
        score = jnp.where(unseen, dot(k, q, (1, 1)), 0.0).astype(BF16)
        edges += [-dot(score, g, (1, 0))[:EDGE], k.astype(F32)[:EDGE]]
    edge_ref[...] = jnp.concatenate(edges, axis=0).astype(BF16)


def lagged(v, halo_ref, head):
    halo = halo_ref[...].astype(F32)[head * EDGE : (head + 1) * EDGE]
    ext = jnp.concatenate([jnp.zeros((TILE - EDGE, DH), F32), halo, v.astype(F32)], axis=0)
    return [ext[TILE - j : TILE - j + v.shape[0]] for j in range(CW)]


def tap_rows(w_ref, core, head):
    return w_ref[:, pl.ds(pl.multiple_of(core * WIDE + head * DH, DH), DH)]


def later(rows):
    first = lax.broadcasted_iota(jnp.int32, (rows, rows), 0)
    return first <= lax.broadcasted_iota(jnp.int32, (rows, rows), 1)


def tap_states(wide_ref, head, k, parts):
    for j, part in enumerate(parts):
        wide_ref[head, j] = dot(k, part.astype(BF16), (0, 0)).astype(BF16)


def add_taps(taps_ref, head, grad, parts):
    for j, part in enumerate(parts):
        row = j * HALF + head
        taps_ref[row : row + 1, :] = jnp.sum(grad * part, axis=0, keepdims=True)


def score_kernel(
    core_ref, q_ref, g_ref, k_ref, v_ref, halo_ref, gc_ref, taps_ref, wide_ref
):
    seen = later(q_ref.shape[0])
    for i in range(HALF):
        at = columns(i)
        k = k_ref[:, at]
        score = jnp.where(seen, dot(k, q_ref[:, at], (1, 1)), 0.0).astype(BF16)
        gc = dot(score, g_ref[:, at], (1, 0))
        gc_ref[:, at] = gc.astype(BF16)
        parts = lagged(v_ref[:, at], halo_ref, i)
        add_taps(taps_ref, i, gc, parts)
        tap_states(wide_ref, i, k, parts)


def convolved(w_ref, core, head, parts):
    taps = tap_rows(w_ref, core, head)
    acc = taps[0:1] * parts[0]
    for j in range(1, CW):
        acc = acc + taps[j : j + 1] * parts[j]
    return acc


def conv_kernel(core_ref, k_ref, v_ref, w_ref, c_ref, state_ref):
    rows = v_ref.shape[0]
    body = lax.broadcasted_iota(jnp.int32, (rows, DH), 0) >= HALO
    for i in range(HALF):
        at = columns(i)
        v = v_ref[:, at].astype(F32)
        ext = jnp.concatenate([jnp.zeros((HALO, DH), F32), v], axis=0)
        parts = [ext[HALO - j : HALO - j + rows] for j in range(CW)]
        c = jnp.where(body, convolved(w_ref, core_ref[0], i, parts), 0.0).astype(BF16)
        c_ref[:, at] = c
        state_ref[i] = dot(k_ref[:, at], c, (0, 0))


def turn_kernel(
    core_ref,
    q_ref,
    state_ref,
    k_ref,
    v_ref,
    halo_ref,
    w_ref,
    out_ref,
    head_ref,
    done_ref,
    *,
    turns,
):
    depth = q_ref.shape[1]
    for i in range(HALF):
        at = columns(i)
        parts = lagged(v_ref[:HALO, at], halo_ref, i)
        c = convolved(w_ref, core_ref[0], i, parts).astype(BF16)
        head_ref[:, at] = c
        state = state_ref[i] + dot(k_ref[:HALO, at], c, (0, 0))
        for n in range(DH // depth):
            part = state[n * depth : (n + 1) * depth].astype(BF16)
            out_ref[i * (DH // depth) + n, 1] = part
    total = jnp.zeros(q_ref.shape[1:], F32)
    for n, slot in reversed(turns):
        out_ref[slot, 0] = total.astype(BF16)
        total = total + q_ref[n].astype(F32)
    done_ref[...] = jnp.zeros(done_ref.shape, F32)


def head_state(read, head, depth):
    parts = DH // depth
    if depth % HALO == 0:
        return jnp.concatenate([read(head * parts + n) for n in range(parts)], axis=0)
    found = [read(head * parts + n).astype(F32) for n in range(parts)]
    return jnp.concatenate(found, axis=0).astype(BF16)


def tap_kernel(
    core_ref,
    chip_ref,
    wide_ref,
    near_ref,
    edge_ref,
    out_ref,
    done_ref,
    taps_ref,
    *,
    scale,
    places,
    ways,
):
    depth = chip_ref.shape[2]
    size = out_ref.shape[1] - CW * HALF
    total = jnp.zeros((depth, DH), F32)
    for n, slot in places:
        out_ref[slot, :depth] = total.astype(BF16)
        if depth < size:
            out_ref[slot, depth:size] = jnp.zeros((size - depth, DH), BF16)
        total = total + chip_ref[n, 1].astype(F32)
    for i in range(HALF):
        suffix = head_state(lambda n: chip_ref[ways[n], 0], i, depth).astype(F32)
        add_taps(taps_ref, i, suffix, [wide_ref[i, j].astype(F32) for j in range(CW)])
    weights = (scale * (near_ref[...] + taps_ref[...])).astype(BF16)
    for n in range(out_ref.shape[0]):
        out_ref[n, size:] = weights
    done_ref[...] = jnp.zeros(done_ref.shape, F32)


def query_side_kernel(
    core_ref,
    chip_ref,
    k_ref,
    g_ref,
    head_ref,
    edge_ref,
    w_ref,
    done_ref,
    c_ref,
    gc_ref,
    q_ref,
    gk_ref,
    gv_ref,
    send_ref,
    gq_ref,
    own_ref,
    hold_ref,
    sems,
    fetch_sems,
    *,
    scale,
    ways,
):
    core = core_ref[0]
    rows = k_ref.shape[0]
    depth = chip_ref.shape[2]
    seen = later(rows)
    fetches = [
        pltpu.make_async_copy(ref, hold_ref.at[n], fetch_sems.at[n])
        for n, ref in enumerate((c_ref, q_ref, gc_ref))
    ]
    for fetch in fetches:
        fetch.start()
    for fetch in fetches:
        fetch.wait()
    for i in range(HALF):
        at = columns(i)
        suffix = head_state(lambda n: chip_ref[ways[n], 0], i, depth)
        c = jnp.concatenate([head_ref[:, at], hold_ref[0, HALO:, at]], axis=0)
        g, k = g_ref[:, at], k_ref[:, at]
        attn = jnp.where(seen.T, dot(g, c, (1, 1)), 0.0)
        gq_ref[:, at] = dot(attn.astype(BF16), k, (1, 0)).astype(BF16)
        turned = jnp.where(seen, dot(c, g, (1, 1)), 0.0)
        gk = dot(turned.astype(BF16), hold_ref[1, :, at], (1, 0))
        gk = scale * (gk + dot(c, suffix, (1, 1)))
        gc = scale * (hold_ref[2, :, at].astype(F32) + dot(k, suffix, (1, 0)))
        edge = edge_ref[...].astype(F32)[2 * EDGE * i : 2 * EDGE * (i + 1)]
        after = edge[:EDGE] + dot(edge.astype(BF16), suffix, (1, 0))[EDGE:]
        ext = jnp.concatenate([gc, scale * after, jnp.zeros((TILE - EDGE, DH), F32)], axis=0)
        taps = tap_rows(w_ref, core, i)
        gv = taps[0:1] * gc
        for j in range(1, CW):
            gv = gv + taps[j : j + 1] * ext[j : j + rows]
        for n, value in enumerate((gk, gv)):
            low, high = value[: rows // 2].astype(BF16), value[rows // 2 :].astype(BF16)
            own_ref[n, :, at] = jnp.where(core == 0, low, high)
            send_ref[n, :, at] = jnp.where(core == 0, high, low)
    put(own_ref, core, (gk_ref, gv_ref), sems)


def put(half_ref, side, refs, sems):
    copies = [
        pltpu.make_async_copy(half_ref.at[n], ref.at[:, half_of(side, WIDE)], sems.at[n])
        for n, ref in enumerate(refs)
    ]
    for copy in copies:
        copy.start()
    for copy in copies:
        copy.wait()


def key_side_kernel(
    core_ref, chip_ref, g_ref, gq_ref, own_ref, send_ref, taps_ref, *, scale, depth, slots
):
    core = core_ref[0]
    rows = g_ref.shape[0]
    chips, size, _ = chip_ref.shape
    for i in range(HALF):
        at = columns(i)
        prefix = head_state(lambda n: chip_ref[slots[n], :depth], i, depth)
        gq = scale * (gq_ref[:, at].astype(F32) + dot(g_ref[:, at], prefix, (1, 1)))
        low, high = gq[: rows // 2].astype(BF16), gq[rows // 2 :].astype(BF16)
        own_ref[:, at] = jnp.where(core == 0, low, high)
        send_ref[:, at] = jnp.where(core == 0, high, low)
    total = chip_ref[0, size - CW * HALF :].astype(F32)
    for n in range(1, chips):
        total = total + chip_ref[n, size - CW * HALF :].astype(F32)
    taps_ref[...] = total


def join_kernel(core_ref, recv_ref, own_ref, _, __, gk_ref, gv_ref, gq_ref, sems, sem):
    core = core_ref[0]
    copy = pltpu.make_async_copy(own_ref, gq_ref.at[:, half_of(core, WIDE)], sem)
    copy.start()
    put(recv_ref, 1 - core, (gk_ref, gv_ref), sems)
    copy.wait()


def finish_kernel(
    core_ref, recv_ref, taps_ref, far_ref, _, gq_ref, gw_ref, hold_ref, sems
):
    core = core_ref[0]
    place = gq_ref.at[:, half_of(1 - core, WIDE)]
    copies = [pltpu.make_async_copy(recv_ref, place, sems.at[0])]
    copies[0].start()
    for side, ref in ((core, taps_ref), (1 - core, far_ref)):
        for i in range(HALF):
            at = pl.ds(pl.multiple_of(side * WIDE + i * DH, DH), DH)
            for j in range(CW):
                row = j * HALF + i
                hold_ref[j : j + 1, at] = ref[row : row + 1, :]
    copies.append(pltpu.make_async_copy(hold_ref, gw_ref, sems.at[1]))
    copies[1].start()
    for copy in copies:
        copy.wait()


def local(queries, keys, values, grad_out, conv_weight):
    rows, width = queries.shape
    lines, line = lax.axis_size("row"), lax.axis_size("col") // 2
    count = 2 * lines * line
    chips = lines * line
    depth = WIDE // chips
    scale = (DH * rows * count) ** (-0.5)
    core = lax.rem(lax.axis_index("col"), 2).astype(jnp.int32).reshape(1)
    half = line // 2
    split = [*reversed(range(half)), *range(half, line)]
    spread = sorted(range(line), key=lambda z: (abs(2 * z + 1 - line), -z))
    mixed = [z for n in range(half) for z in (half + n, n)]
    lists = [
        [r * line + z for r in reversed(range(lines)) for z in along]
        for along in (split, spread, mixed)
    ]
    groups = [[[2 * p + c for p in each] for c in range(2)] for each in lists]
    spots = [[each.index(p) for p in range(chips)] for each in lists]
    turns = tuple(zip(spots[0], spots[1]))
    places = tuple(zip(spots[1], spots[2]))
    ways = tuple(spots[1][p] for p in lists[0])
    slots = tuple(spots[2][p] for p in lists[1])

    def swap(value):
        return lax.ppermute(value, AXES, [(d, d ^ 1) for d in range(count)])

    def shifted(value, by):
        pairs = [(d, d + by) for d in range(count) if 0 <= d + by < count]
        return lax.ppermute(value, AXES, pairs)

    def turn(value, groups):
        return lax.all_to_all(value, AXES, 0, 0, axis_index_groups=groups, tiled=True)

    pair = shape((2, rows, WIDE))
    block = shape((2 * rows, WIDE))
    far_block = pltpu.HBM((2 * rows, WIDE), BF16)
    states = shape((HALF, DH, DH))
    edges = shape((HALO, WIDE))
    flag = shape((8, DH), F32)
    dma = pltpu.SemaphoreType.DMA
    padded = max(depth, HALO)

    def in_hbm(value):
        return pltpu.with_memory_space_constraint(value, pltpu.HBM)

    queries, grad_out, keys, values = map(in_hbm, (queries, grad_out, keys, values))
    q_keep, q_give = call(
        query_state_kernel,
        (states, states),
        core,
        [queries, grad_out],
        [pltpu.VMEM((2, rows, width), BF16), dma((2,))],
        [ANY] * 2,
    )
    q_recv = swap(q_give)
    longer = shape((2, rows + HALO, WIDE))
    kv_own, kv_send = call(
        split_key_kernel,
        (longer, longer),
        core,
        [keys, values, queries, grad_out, q_keep],
        [dma((2, 2, 2))],
        [ANY] * 4 + [VMEM],
    )
    kv_recv = swap(kv_send)
    q_sent, added = call(
        add_kernel,
        (states, flag),
        core,
        [q_keep, q_recv],
    )
    q_turned = turn(q_sent.reshape(chips, depth, DH), groups[0])
    qg_own, qg_send = call(
        split_kernel,
        (pair, pair),
        core,
        [queries, grad_out, added],
        [dma((2, 2))],
        [ANY, ANY, VMEM],
    )
    qg_recv = swap(qg_send)
    tail = call(tail_kernel, shape((EDGE * HALF, DH)), core, [kv_own, kv_recv])
    k, v, edge = call(
        gather_key_kernel,
        (block, block, shape((2 * EDGE * HALF, DH))),
        core,
        [kv_own, kv_recv],
    )
    halo = shifted(tail, 2)
    q, g, q_far = call(
        gather_query_kernel,
        (block, block, far_block),
        core,
        [qg_own, qg_recv],
        [dma(())],
        made=(VMEM, VMEM, ANY),
    )
    c, k_state = call(
        conv_kernel,
        (far_block, shape((HALF, DH, DH), F32)),
        core,
        [k, v, conv_weight],
    )
    both, c_head, turned = call(
        functools.partial(turn_kernel, turns=turns),
        (shape((chips, 2, depth, DH)), edges, flag),
        core,
        [q_turned, k_state, k, v, halo, conv_weight],
    )
    both = turn(both, groups[1])
    gc, taps, wide = call(
        score_kernel,
        (far_block, shape((CW * HALF, DH), F32), shape((HALF, CW, DH, DH))),
        core,
        [q, g, k, v, halo]
    )
    edge = shifted(edge, -2)
    last, tapped = call(
        functools.partial(tap_kernel, scale=scale, places=places, ways=ways),
        (shape((chips, padded + CW * HALF, DH)), flag),
        core,
        [both, wide, taps, edge],
        [pltpu.VMEM((CW * HALF, DH), F32)],
    )
    last = turn(last, groups[2])
    full = shape((rows, width))
    grad_keys, grad_values, kv_give, gq = call(
        functools.partial(query_side_kernel, scale=scale, ways=ways),
        (full, full, pair, block),
        core,
        [both, k, g, c_head, edge, conv_weight, tapped, *map(in_hbm, (c, gc, q_far))],
        [pltpu.VMEM((2, rows, WIDE), BF16), pltpu.VMEM((3, 2 * rows, WIDE), BF16)]
        + [dma((2,)), dma((3,))],
        [VMEM] * 7 + [ANY] * 3,
        (ANY, ANY, VMEM, VMEM),
    )
    kv_got = swap(kv_give)
    q_grad, q_give, taps = call(
        functools.partial(key_side_kernel, scale=scale, depth=depth, slots=slots),
        (shape((rows, WIDE)), shape((rows, WIDE)), shape((CW * HALF, DH), F32)),
        core,
        [last, g, gq],
    )
    q_got = swap(q_give)
    far = swap(taps)
    grad_keys, grad_values, grad_queries = call(
        join_kernel,
        (full, full, full),
        core,
        [kv_got, q_grad, grad_keys, grad_values],
        [dma((2,)), dma(())],
        [VMEM, VMEM, ANY, ANY],
        (ANY, ANY, ANY),
        {3: 0, 4: 1},
    )
    grad_queries, grad_weight = call(
        finish_kernel,
        (full, shape((CW, width), F32)),
        core,
        [q_got, taps, far, grad_queries],
        [pltpu.VMEM((CW, width), F32), dma((2,))],
        [VMEM, VMEM, VMEM, ANY],
        (ANY, ANY),
        {4: 0},
    )
    return grad_queries, grad_keys, grad_values, grad_weight


def solution(mesh):
    placed = (
        P(("row", "col"), None),
        P(("row", "col"), None),
        P(("row", "col"), None),
        P(("row", "col"), None),
        P(),
    )
    return jax.shard_map(
        local,
        mesh=mesh,
        in_specs=placed,
        out_specs=(P(("row", "col"), None), P(("row", "col"), None), P(("row", "col"), None), P()),
        check_vma=False,
    )
```

```python
import functools

import jax
import jax.numpy as jnp
from jax import lax
from jax.experimental import pallas as pl
from jax.experimental.pallas import tpu as pltpu
from jax.sharding import PartitionSpec as P

HEADS = 16
DH = 128
CW = 4
HALF = HEADS // 2
WIDE = HALF * DH
EDGE = 4
TILE = 8
HALO = 16
AXES = ("row", "col")
F32 = jnp.float32
BF16 = jnp.bfloat16
VMEM = pl.BlockSpec(memory_space=pltpu.VMEM)
SMEM = pl.BlockSpec(memory_space=pltpu.SMEM)
ANY = pl.BlockSpec(memory_space=pl.ANY)
PARAMS = pltpu.CompilerParams(vmem_limit_bytes=16 * 1024 * 1024)


def dot(a, b, over):
    return lax.dot_general(a, b, ((over[:1], over[1:]), ((), ())), preferred_element_type=F32)


def columns(head):
    return pl.ds(head * DH, DH)


def half_of(core, size):
    return pl.ds(pl.multiple_of(core * size, size), size)


def call(kernel, outs, core, arrays, scratch=(), given=None, made=None, aliases={}):
    return pl.pallas_call(
        kernel,
        out_shape=outs,
        in_specs=[SMEM] + (given or [VMEM] * len(arrays)),
        out_specs=made or jax.tree.map(lambda _: VMEM, outs),
        scratch_shapes=scratch,
        input_output_aliases=aliases,
        compiler_params=PARAMS,
    )(core, *arrays)


def shape(dims, dtype=BF16):
    return jax.ShapeDtypeStruct(dims, dtype)


def split_key_kernel(
    core_ref, k_ref, v_ref, q_ref, g_ref, after_ref, own_ref, send_ref, sems
):
    core = core_ref[0]
    rows = k_ref.shape[0]
    copies = []
    for n, refs in enumerate(((k_ref, q_ref), (v_ref, g_ref))):
        for m, (out, side) in enumerate(((send_ref, 1 - core), (own_ref, core))):
            for e, (ref, first, size) in enumerate(zip(refs, (0, rows), (rows, HALO))):
                part = ref.at[pl.ds(0, size), half_of(side, WIDE)]
                place = out.at[n, pl.ds(first, size)]
                copies.append(pltpu.make_async_copy(part, place, sems.at[n, m, e]))
    for copy in copies:
        copy.start()
    for copy in copies:
        copy.wait()


def split_kernel(core_ref, a_ref, b_ref, after_ref, own_ref, send_ref, sems):
    core = core_ref[0]
    copies = []
    for n, ref in enumerate((a_ref, b_ref)):
        for m, (out, side) in enumerate(((send_ref, 1 - core), (own_ref, core))):
            copies.append(
                pltpu.make_async_copy(ref.at[:, half_of(side, WIDE)], out.at[n], sems.at[n, m])
            )
    for copy in copies:
        copy.start()
    for copy in copies:
        copy.wait()


def query_state_kernel(
    core_ref, q_ref, g_ref, keep_ref, give_ref, held_ref, sems
):
    core = core_ref[0]
    copies = [
        pltpu.make_async_copy(ref, held_ref.at[n], sems.at[n])
        for n, ref in enumerate((q_ref, g_ref))
    ]
    for copy in copies:
        copy.start()
    for copy in copies:
        copy.wait()
    for side, out in ((1 - core, give_ref), (core, keep_ref)):
        for i in range(HALF):
            at = pl.ds(pl.multiple_of(side * WIDE + i * DH, DH), DH)
            out[i] = dot(held_ref[0, :, at], held_ref[1, :, at], (0, 0)).astype(BF16)


def add_kernel(core_ref, keep_ref, recv_ref, out_ref, done_ref):
    for i in range(HALF):
        out_ref[i] = (keep_ref[i].astype(F32) + recv_ref[i].astype(F32)).astype(BF16)
    done_ref[...] = jnp.zeros(done_ref.shape, F32)


def gather(core, own_ref, recv_ref, refs):
    for n, ref in enumerate(refs):
        rows = ref.shape[0] // 2
        ref[half_of(core, rows), :] = own_ref[n, :rows]
        ref[half_of(1 - core, rows), :] = recv_ref[n, :rows]


def gather_query_kernel(core_ref, own_ref, recv_ref, q_ref, g_ref, far_ref, sem):
    gather(core_ref[0], own_ref, recv_ref, (q_ref, g_ref))
    copy = pltpu.make_async_copy(q_ref, far_ref, sem)
    copy.start()
    copy.wait()


def tail_kernel(core_ref, own_ref, recv_ref, tail_ref):
    rows = own_ref.shape[1] - HALO
    tails = []
    for i in range(HALF):
        at = columns(i)
        own, recv = (ref[1, rows - HALO : rows, at] for ref in (own_ref, recv_ref))
        tail = jnp.where(core_ref[0] == 1, own, recv)
        tails.append(tail.astype(F32)[HALO - EDGE :])
    tail_ref[...] = jnp.concatenate(tails, axis=0).astype(BF16)


def gather_key_kernel(core_ref, own_ref, recv_ref, k_ref, v_ref, edge_ref):
    core = core_ref[0]
    gather(core, own_ref, recv_ref, (k_ref, v_ref))
    rows = k_ref.shape[0]
    edges = []
    first = lax.broadcasted_iota(jnp.int32, (HALO, HALO), 0)
    unseen = first > lax.broadcasted_iota(jnp.int32, (HALO, HALO), 1)
    for i in range(HALF):
        at = columns(i)
        q, g = (
            jnp.where(core == 0, own_ref[n, rows // 2 :, at], recv_ref[n, rows // 2 :, at])
            for n in range(2)
        )
        k = k_ref[:HALO, at]
        score = jnp.where(unseen, dot(k, q, (1, 1)), 0.0).astype(BF16)
        edges += [-dot(score, g, (1, 0))[:EDGE], k.astype(F32)[:EDGE]]
    edge_ref[...] = jnp.concatenate(edges, axis=0).astype(BF16)


def lagged(v, halo_ref, head):
    halo = halo_ref[...].astype(F32)[head * EDGE : (head + 1) * EDGE]
    ext = jnp.concatenate([jnp.zeros((TILE - EDGE, DH), F32), halo, v.astype(F32)], axis=0)
    return [ext[TILE - j : TILE - j + v.shape[0]] for j in range(CW)]


def tap_rows(w_ref, core, head):
    return w_ref[:, pl.ds(pl.multiple_of(core * WIDE + head * DH, DH), DH)]


def later(rows):
    first = lax.broadcasted_iota(jnp.int32, (rows, rows), 0)
    return first <= lax.broadcasted_iota(jnp.int32, (rows, rows), 1)


def tap_states(wide_ref, head, k, parts):
    for j, part in enumerate(parts):
        wide_ref[head, j] = dot(k, part.astype(BF16), (0, 0)).astype(BF16)


def add_taps(taps_ref, head, grad, parts):
    for j, part in enumerate(parts):
        row = j * HALF + head
        taps_ref[row : row + 1, :] = jnp.sum(grad * part, axis=0, keepdims=True)


def score_kernel(
    core_ref, q_ref, g_ref, k_ref, v_ref, halo_ref, gc_ref, taps_ref, wide_ref
):
    seen = later(q_ref.shape[0])
    for i in range(HALF):
        at = columns(i)
        k = k_ref[:, at]
        score = jnp.where(seen, dot(k, q_ref[:, at], (1, 1)), 0.0).astype(BF16)
        gc = dot(score, g_ref[:, at], (1, 0))
        gc_ref[:, at] = gc.astype(BF16)
        parts = lagged(v_ref[:, at], halo_ref, i)
        add_taps(taps_ref, i, gc, parts)
        tap_states(wide_ref, i, k, parts)


def convolved(w_ref, core, head, parts):
    taps = tap_rows(w_ref, core, head)
    acc = taps[0:1] * parts[0]
    for j in range(1, CW):
        acc = acc + taps[j : j + 1] * parts[j]
    return acc


def conv_kernel(core_ref, k_ref, v_ref, w_ref, c_ref, state_ref):
    rows = v_ref.shape[0]
    body = lax.broadcasted_iota(jnp.int32, (rows, DH), 0) >= HALO
    for i in range(HALF):
        at = columns(i)
        v = v_ref[:, at].astype(F32)
        ext = jnp.concatenate([jnp.zeros((HALO, DH), F32), v], axis=0)
        parts = [ext[HALO - j : HALO - j + rows] for j in range(CW)]
        c = jnp.where(body, convolved(w_ref, core_ref[0], i, parts), 0.0).astype(BF16)
        c_ref[:, at] = c
        state_ref[i] = dot(k_ref[:, at], c, (0, 0))


def turn_kernel(
    core_ref,
    q_ref,
    state_ref,
    k_ref,
    v_ref,
    halo_ref,
    w_ref,
    after_ref,
    out_ref,
    head_ref,
    done_ref,
    *,
    turns,
):
    depth = q_ref.shape[1]
    for i in range(HALF):
        at = columns(i)
        parts = lagged(v_ref[:HALO, at], halo_ref, i)
        c = convolved(w_ref, core_ref[0], i, parts).astype(BF16)
        head_ref[:, at] = c
        state = state_ref[i] + dot(k_ref[:HALO, at], c, (0, 0))
        for n in range(DH // depth):
            part = state[n * depth : (n + 1) * depth].astype(BF16)
            out_ref[i * (DH // depth) + n, 1] = part
    total = jnp.zeros(q_ref.shape[1:], F32)
    for n, slot in reversed(turns):
        out_ref[slot, 0] = total.astype(BF16)
        total = total + q_ref[n].astype(F32)
    done_ref[...] = jnp.zeros(done_ref.shape, F32)


def head_state(read, head, depth):
    parts = DH // depth
    if depth % HALO == 0:
        return jnp.concatenate([read(head * parts + n) for n in range(parts)], axis=0)
    found = [read(head * parts + n).astype(F32) for n in range(parts)]
    return jnp.concatenate(found, axis=0).astype(BF16)


def tap_kernel(
    core_ref,
    chip_ref,
    wide_ref,
    near_ref,
    edge_ref,
    out_ref,
    done_ref,
    taps_ref,
    *,
    scale,
    places,
    ways,
):
    depth = chip_ref.shape[2]
    size = out_ref.shape[1] - CW * HALF
    total = jnp.zeros((depth, DH), F32)
    for n, slot in places:
        out_ref[slot, :depth] = total.astype(BF16)
        if depth < size:
            out_ref[slot, depth:size] = jnp.zeros((size - depth, DH), BF16)
        total = total + chip_ref[n, 1].astype(F32)
    for i in range(HALF):
        suffix = head_state(lambda n: chip_ref[ways[n], 0], i, depth).astype(F32)
        add_taps(taps_ref, i, suffix, [wide_ref[i, j].astype(F32) for j in range(CW)])
    weights = (scale * (near_ref[...] + taps_ref[...])).astype(BF16)
    for n in range(out_ref.shape[0]):
        out_ref[n, size:] = weights
    done_ref[...] = jnp.zeros(done_ref.shape, F32)


def query_side_kernel(
    core_ref,
    chip_ref,
    k_ref,
    g_ref,
    head_ref,
    edge_ref,
    w_ref,
    done_ref,
    c_ref,
    gc_ref,
    q_ref,
    gk_ref,
    gv_ref,
    send_ref,
    gq_ref,
    own_ref,
    hold_ref,
    sems,
    fetch_sems,
    *,
    scale,
    ways,
):
    core = core_ref[0]
    rows = k_ref.shape[0]
    depth = chip_ref.shape[2]
    seen = later(rows)
    fetches = [
        pltpu.make_async_copy(ref, hold_ref.at[n], fetch_sems.at[n])
        for n, ref in enumerate((c_ref, q_ref, gc_ref))
    ]
    for fetch in fetches:
        fetch.start()
    for fetch in fetches:
        fetch.wait()
    for i in range(HALF):
        at = columns(i)
        suffix = head_state(lambda n: chip_ref[ways[n], 0], i, depth)
        c = jnp.concatenate([head_ref[:, at], hold_ref[0, HALO:, at]], axis=0)
        g, k = g_ref[:, at], k_ref[:, at]
        attn = jnp.where(seen.T, dot(g, c, (1, 1)), 0.0)
        gq_ref[:, at] = dot(attn.astype(BF16), k, (1, 0)).astype(BF16)
        turned = jnp.where(seen, dot(c, g, (1, 1)), 0.0)
        gk = dot(turned.astype(BF16), hold_ref[1, :, at], (1, 0))
        gk = scale * (gk + dot(c, suffix, (1, 1)))
        gc = scale * (hold_ref[2, :, at].astype(F32) + dot(k, suffix, (1, 0)))
        edge = edge_ref[...].astype(F32)[2 * EDGE * i : 2 * EDGE * (i + 1)]
        after = edge[:EDGE] + dot(edge.astype(BF16), suffix, (1, 0))[EDGE:]
        ext = jnp.concatenate([gc, scale * after, jnp.zeros((TILE - EDGE, DH), F32)], axis=0)
        taps = tap_rows(w_ref, core, i)
        gv = taps[0:1] * gc
        for j in range(1, CW):
            gv = gv + taps[j : j + 1] * ext[j : j + rows]
        for n, value in enumerate((gk, gv)):
            low, high = value[: rows // 2].astype(BF16), value[rows // 2 :].astype(BF16)
            own_ref[n, :, at] = jnp.where(core == 0, low, high)
            send_ref[n, :, at] = jnp.where(core == 0, high, low)
    put(own_ref, core, (gk_ref, gv_ref), sems)


def put(half_ref, side, refs, sems):
    copies = [
        pltpu.make_async_copy(half_ref.at[n], ref.at[:, half_of(side, WIDE)], sems.at[n])
        for n, ref in enumerate(refs)
    ]
    for copy in copies:
        copy.start()
    for copy in copies:
        copy.wait()


def key_side_kernel(
    core_ref, chip_ref, g_ref, gq_ref, own_ref, send_ref, taps_ref, *, scale, depth, slots
):
    core = core_ref[0]
    rows = g_ref.shape[0]
    chips, size, _ = chip_ref.shape
    for i in range(HALF):
        at = columns(i)
        prefix = head_state(lambda n: chip_ref[slots[n], :depth], i, depth)
        gq = scale * (gq_ref[:, at].astype(F32) + dot(g_ref[:, at], prefix, (1, 1)))
        low, high = gq[: rows // 2].astype(BF16), gq[rows // 2 :].astype(BF16)
        own_ref[:, at] = jnp.where(core == 0, low, high)
        send_ref[:, at] = jnp.where(core == 0, high, low)
    total = chip_ref[0, size - CW * HALF :].astype(F32)
    for n in range(1, chips):
        total = total + chip_ref[n, size - CW * HALF :].astype(F32)
    taps_ref[...] = total


def join_kernel(core_ref, recv_ref, own_ref, _, __, gk_ref, gv_ref, gq_ref, sems, sem):
    core = core_ref[0]
    copy = pltpu.make_async_copy(own_ref, gq_ref.at[:, half_of(core, WIDE)], sem)
    copy.start()
    put(recv_ref, 1 - core, (gk_ref, gv_ref), sems)
    copy.wait()


def finish_kernel(
    core_ref, recv_ref, taps_ref, far_ref, _, gq_ref, gw_ref, hold_ref, sems
):
    core = core_ref[0]
    place = gq_ref.at[:, half_of(1 - core, WIDE)]
    copies = [pltpu.make_async_copy(recv_ref, place, sems.at[0])]
    copies[0].start()
    for side, ref in ((core, taps_ref), (1 - core, far_ref)):
        for i in range(HALF):
            at = pl.ds(pl.multiple_of(side * WIDE + i * DH, DH), DH)
            for j in range(CW):
                row = j * HALF + i
                hold_ref[j : j + 1, at] = ref[row : row + 1, :]
    copies.append(pltpu.make_async_copy(hold_ref, gw_ref, sems.at[1]))
    copies[1].start()
    for copy in copies:
        copy.wait()


def local(queries, keys, values, grad_out, conv_weight):
    rows, width = queries.shape
    lines, line = lax.axis_size("row"), lax.axis_size("col") // 2
    count = 2 * lines * line
    chips = lines * line
    depth = WIDE // chips
    scale = (DH * rows * count) ** (-0.5)
    core = lax.rem(lax.axis_index("col"), 2).astype(jnp.int32).reshape(1)
    half = line // 2
    split = [*reversed(range(half)), *range(half, line)]
    spread = sorted(range(line), key=lambda z: (abs(2 * z + 1 - line), -z))
    mixed = [z for n in range(half) for z in (half + n, n)]
    lists = [
        [r * line + z for r in reversed(range(lines)) for z in along]
        for along in (split, spread, mixed)
    ]
    groups = [[[2 * p + c for p in each] for c in range(2)] for each in lists]
    spots = [[each.index(p) for p in range(chips)] for each in lists]
    turns = tuple(zip(spots[0], spots[1]))
    places = tuple(zip(spots[1], spots[2]))
    ways = tuple(spots[1][p] for p in lists[0])
    slots = tuple(spots[2][p] for p in lists[1])

    def swap(value):
        return lax.ppermute(value, AXES, [(d, d ^ 1) for d in range(count)])

    def shifted(value, by):
        pairs = [(d, d + by) for d in range(count) if 0 <= d + by < count]
        return lax.ppermute(value, AXES, pairs)

    def turn(value, groups):
        return lax.all_to_all(value, AXES, 0, 0, axis_index_groups=groups, tiled=True)

    pair = shape((2, rows, WIDE))
    block = shape((2 * rows, WIDE))
    far_block = pltpu.HBM((2 * rows, WIDE), BF16)
    states = shape((HALF, DH, DH))
    edges = shape((HALO, WIDE))
    flag = shape((8, DH), F32)
    dma = pltpu.SemaphoreType.DMA
    padded = max(depth, HALO)

    def in_hbm(value):
        return pltpu.with_memory_space_constraint(value, pltpu.HBM)

    queries, grad_out, keys, values = map(in_hbm, (queries, grad_out, keys, values))
    q_keep, q_give = call(
        query_state_kernel,
        (states, states),
        core,
        [queries, grad_out],
        [pltpu.VMEM((2, rows, width), BF16), dma((2,))],
        [ANY] * 2,
    )
    q_recv = swap(q_give)
    longer = shape((2, rows + HALO, WIDE))
    kv_own, kv_send = call(
        split_key_kernel,
        (longer, longer),
        core,
        [keys, values, queries, grad_out, q_keep],
        [dma((2, 2, 2))],
        [ANY] * 4 + [VMEM],
    )
    kv_recv = swap(kv_send)
    q_sent, added = call(
        add_kernel,
        (states, flag),
        core,
        [q_keep, q_recv],
    )
    q_turned = turn(q_sent.reshape(chips, depth, DH), groups[0])
    tail = call(tail_kernel, shape((EDGE * HALF, DH)), core, [kv_own, kv_recv])
    k, v, edge = call(
        gather_key_kernel,
        (block, block, shape((2 * EDGE * HALF, DH))),
        core,
        [kv_own, kv_recv],
    )
    halo = shifted(tail, 2)
    c, k_state = call(
        conv_kernel,
        (far_block, shape((HALF, DH, DH), F32)),
        core,
        [k, v, conv_weight],
    )
    qg_own, qg_send = call(
        split_kernel,
        (pair, pair),
        core,
        [queries, grad_out, k_state],
        [dma((2, 2))],
        [ANY, ANY, VMEM],
    )
    qg_recv = swap(qg_send)
    q, g, q_far = call(
        gather_query_kernel,
        (block, block, far_block),
        core,
        [qg_own, qg_recv],
        [dma(())],
        made=(VMEM, VMEM, ANY),
    )
    both, c_head, turned = call(
        functools.partial(turn_kernel, turns=turns),
        (shape((chips, 2, depth, DH)), edges, flag),
        core,
        [q_turned, k_state, k, v, halo, conv_weight, qg_own],
    )
    both = turn(both, groups[1])
    gc, taps, wide = call(
        score_kernel,
        (far_block, shape((CW * HALF, DH), F32), shape((HALF, CW, DH, DH))),
        core,
        [q, g, k, v, halo]
    )
    edge = shifted(edge, -2)
    last, tapped = call(
        functools.partial(tap_kernel, scale=scale, places=places, ways=ways),
        (shape((chips, padded + CW * HALF, DH)), flag),
        core,
        [both, wide, taps, edge],
        [pltpu.VMEM((CW * HALF, DH), F32)],
    )
    last = turn(last, groups[2])
    full = shape((rows, width))
    grad_keys, grad_values, kv_give, gq = call(
        functools.partial(query_side_kernel, scale=scale, ways=ways),
        (full, full, pair, block),
        core,
        [both, k, g, c_head, edge, conv_weight, tapped, *map(in_hbm, (c, gc, q_far))],
        [pltpu.VMEM((2, rows, WIDE), BF16), pltpu.VMEM((3, 2 * rows, WIDE), BF16)]
        + [dma((2,)), dma((3,))],
        [VMEM] * 7 + [ANY] * 3,
        (ANY, ANY, VMEM, VMEM),
    )
    kv_got = swap(kv_give)
    q_grad, q_give, taps = call(
        functools.partial(key_side_kernel, scale=scale, depth=depth, slots=slots),
        (shape((rows, WIDE)), shape((rows, WIDE)), shape((CW * HALF, DH), F32)),
        core,
        [last, g, gq],
    )
    q_got = swap(q_give)
    far = swap(taps)
    grad_keys, grad_values, grad_queries = call(
        join_kernel,
        (full, full, full),
        core,
        [kv_got, q_grad, grad_keys, grad_values],
        [dma((2,)), dma(())],
        [VMEM, VMEM, ANY, ANY],
        (ANY, ANY, ANY),
        {3: 0, 4: 1},
    )
    grad_queries, grad_weight = call(
        finish_kernel,
        (full, shape((CW, width), F32)),
        core,
        [q_got, taps, far, grad_queries],
        [pltpu.VMEM((CW, width), F32), dma((2,))],
        [VMEM, VMEM, VMEM, ANY],
        (ANY, ANY),
        {4: 0},
    )
    return grad_queries, grad_keys, grad_values, grad_weight


def solution(mesh):
    placed = (
        P(("row", "col"), None),
        P(("row", "col"), None),
        P(("row", "col"), None),
        P(("row", "col"), None),
        P(),
    )
    return jax.shard_map(
        local,
        mesh=mesh,
        in_specs=placed,
        out_specs=(P(("row", "col"), None), P(("row", "col"), None), P(("row", "col"), None), P()),
        check_vma=False,
    )
```

```python
import functools

import jax
import jax.numpy as jnp
from jax import lax
from jax.experimental import pallas as pl
from jax.experimental.pallas import tpu as pltpu
from jax.sharding import PartitionSpec as P

HEADS = 16
DH = 128
CW = 4
HALF = HEADS // 2
WIDE = HALF * DH
EDGE = 4
TILE = 8
HALO = 16
AXES = ("row", "col")
F32 = jnp.float32
BF16 = jnp.bfloat16
VMEM = pl.BlockSpec(memory_space=pltpu.VMEM)
SMEM = pl.BlockSpec(memory_space=pltpu.SMEM)
ANY = pl.BlockSpec(memory_space=pl.ANY)
PARAMS = pltpu.CompilerParams(vmem_limit_bytes=16 * 1024 * 1024)


def dot(a, b, over):
    return lax.dot_general(a, b, ((over[:1], over[1:]), ((), ())), preferred_element_type=F32)


def columns(head):
    return pl.ds(head * DH, DH)


def half_of(core, size):
    return pl.ds(pl.multiple_of(core * size, size), size)


def call(kernel, outs, core, arrays, scratch=(), given=None, made=None, aliases={}):
    return pl.pallas_call(
        kernel,
        out_shape=outs,
        in_specs=[SMEM] + (given or [VMEM] * len(arrays)),
        out_specs=made or jax.tree.map(lambda _: VMEM, outs),
        scratch_shapes=scratch,
        input_output_aliases=aliases,
        compiler_params=PARAMS,
    )(core, *arrays)


def shape(dims, dtype=BF16):
    return jax.ShapeDtypeStruct(dims, dtype)


def split_key_kernel(
    core_ref, k_ref, v_ref, q_ref, g_ref, after_ref, own_ref, send_ref, sems
):
    core = core_ref[0]
    rows = k_ref.shape[0]
    copies = []
    for n, refs in enumerate(((k_ref, q_ref), (v_ref, g_ref))):
        for m, (out, side) in enumerate(((send_ref, 1 - core), (own_ref, core))):
            for e, (ref, first, size) in enumerate(zip(refs, (0, rows), (rows, HALO))):
                part = ref.at[pl.ds(0, size), half_of(side, WIDE)]
                place = out.at[n, pl.ds(first, size)]
                copies.append(pltpu.make_async_copy(part, place, sems.at[n, m, e]))
    for copy in copies:
        copy.start()
    for copy in copies:
        copy.wait()


def split_kernel(core_ref, a_ref, b_ref, after_ref, own_ref, send_ref, sems):
    core = core_ref[0]
    copies = []
    for n, ref in enumerate((a_ref, b_ref)):
        for m, (out, side) in enumerate(((send_ref, 1 - core), (own_ref, core))):
            copies.append(
                pltpu.make_async_copy(ref.at[:, half_of(side, WIDE)], out.at[n], sems.at[n, m])
            )
    for copy in copies:
        copy.start()
    for copy in copies:
        copy.wait()


def query_state_kernel(
    core_ref, q_ref, g_ref, keep_ref, give_ref, held_ref, sems
):
    core = core_ref[0]
    copies = [
        pltpu.make_async_copy(ref, held_ref.at[n], sems.at[n])
        for n, ref in enumerate((q_ref, g_ref))
    ]
    for copy in copies:
        copy.start()
    for copy in copies:
        copy.wait()
    for side, out in ((1 - core, give_ref), (core, keep_ref)):
        for i in range(HALF):
            at = pl.ds(pl.multiple_of(side * WIDE + i * DH, DH), DH)
            out[i] = dot(held_ref[0, :, at], held_ref[1, :, at], (0, 0)).astype(BF16)


def add_kernel(core_ref, keep_ref, recv_ref, out_ref, done_ref):
    for i in range(HALF):
        out_ref[i] = (keep_ref[i].astype(F32) + recv_ref[i].astype(F32)).astype(BF16)
    done_ref[...] = jnp.zeros(done_ref.shape, F32)


def gather(core, own_ref, recv_ref, refs):
    for n, ref in enumerate(refs):
        rows = ref.shape[0] // 2
        ref[half_of(core, rows), :] = own_ref[n, :rows]
        ref[half_of(1 - core, rows), :] = recv_ref[n, :rows]


def gather_query_kernel(core_ref, own_ref, recv_ref, q_ref, g_ref, far_ref, sem):
    gather(core_ref[0], own_ref, recv_ref, (q_ref, g_ref))
    copy = pltpu.make_async_copy(q_ref, far_ref, sem)
    copy.start()
    copy.wait()


def tail_kernel(core_ref, own_ref, recv_ref, tail_ref):
    rows = own_ref.shape[1] - HALO
    tails = []
    for i in range(HALF):
        at = columns(i)
        own, recv = (ref[1, rows - HALO : rows, at] for ref in (own_ref, recv_ref))
        tail = jnp.where(core_ref[0] == 1, own, recv)
        tails.append(tail.astype(F32)[HALO - EDGE :])
    tail_ref[...] = jnp.concatenate(tails, axis=0).astype(BF16)


def gather_key_kernel(core_ref, own_ref, recv_ref, k_ref, v_ref, edge_ref):
    core = core_ref[0]
    gather(core, own_ref, recv_ref, (k_ref, v_ref))
    rows = k_ref.shape[0]
    edges = []
    first = lax.broadcasted_iota(jnp.int32, (HALO, HALO), 0)
    unseen = first > lax.broadcasted_iota(jnp.int32, (HALO, HALO), 1)
    for i in range(HALF):
        at = columns(i)
        q, g = (
            jnp.where(core == 0, own_ref[n, rows // 2 :, at], recv_ref[n, rows // 2 :, at])
            for n in range(2)
        )
        k = k_ref[:HALO, at]
        score = jnp.where(unseen, dot(k, q, (1, 1)), 0.0).astype(BF16)
        edges += [-dot(score, g, (1, 0))[:EDGE], k.astype(F32)[:EDGE]]
    edge_ref[...] = jnp.concatenate(edges, axis=0).astype(BF16)


def lagged(v, halo_ref, head):
    halo = halo_ref[...].astype(F32)[head * EDGE : (head + 1) * EDGE]
    ext = jnp.concatenate([jnp.zeros((TILE - EDGE, DH), F32), halo, v.astype(F32)], axis=0)
    return [ext[TILE - j : TILE - j + v.shape[0]] for j in range(CW)]


def tap_rows(w_ref, core, head):
    return w_ref[:, pl.ds(pl.multiple_of(core * WIDE + head * DH, DH), DH)]


def later(rows):
    first = lax.broadcasted_iota(jnp.int32, (rows, rows), 0)
    return first <= lax.broadcasted_iota(jnp.int32, (rows, rows), 1)


def tap_states(wide_ref, head, k, parts):
    for j, part in enumerate(parts):
        wide_ref[head, j] = dot(k, part.astype(BF16), (0, 0)).astype(BF16)


def add_taps(taps_ref, head, grad, parts):
    for j, part in enumerate(parts):
        row = j * HALF + head
        taps_ref[row : row + 1, :] = jnp.sum(grad * part, axis=0, keepdims=True)


def score_kernel(
    core_ref, q_ref, g_ref, k_ref, v_ref, halo_ref, gc_ref, taps_ref, wide_ref
):
    seen = later(q_ref.shape[0])
    for i in range(HALF):
        at = columns(i)
        k = k_ref[:, at]
        score = jnp.where(seen, dot(k, q_ref[:, at], (1, 1)), 0.0).astype(BF16)
        gc = dot(score, g_ref[:, at], (1, 0))
        gc_ref[:, at] = gc.astype(BF16)
        parts = lagged(v_ref[:, at], halo_ref, i)
        add_taps(taps_ref, i, gc, parts)
        tap_states(wide_ref, i, k, parts)


def convolved(w_ref, core, head, parts):
    taps = tap_rows(w_ref, core, head)
    acc = taps[0:1] * parts[0]
    for j in range(1, CW):
        acc = acc + taps[j : j + 1] * parts[j]
    return acc


def conv_kernel(core_ref, k_ref, v_ref, w_ref, c_ref, state_ref):
    rows = v_ref.shape[0]
    body = lax.broadcasted_iota(jnp.int32, (rows, DH), 0) >= HALO
    for i in range(HALF):
        at = columns(i)
        v = v_ref[:, at].astype(F32)
        ext = jnp.concatenate([jnp.zeros((HALO, DH), F32), v], axis=0)
        parts = [ext[HALO - j : HALO - j + rows] for j in range(CW)]
        c = jnp.where(body, convolved(w_ref, core_ref[0], i, parts), 0.0).astype(BF16)
        c_ref[:, at] = c
        state_ref[i] = dot(k_ref[:, at], c, (0, 0))


def turn_kernel(
    core_ref,
    q_ref,
    state_ref,
    k_ref,
    v_ref,
    halo_ref,
    w_ref,
    after_ref,
    out_ref,
    head_ref,
    done_ref,
    *,
    turns,
):
    depth = q_ref.shape[1]
    for i in range(HALF):
        at = columns(i)
        parts = lagged(v_ref[:HALO, at], halo_ref, i)
        c = convolved(w_ref, core_ref[0], i, parts).astype(BF16)
        head_ref[:, at] = c
        state = state_ref[i] + dot(k_ref[:HALO, at], c, (0, 0))
        for n in range(DH // depth):
            part = state[n * depth : (n + 1) * depth].astype(BF16)
            out_ref[i * (DH // depth) + n, 1] = part
    total = jnp.zeros(q_ref.shape[1:], F32)
    for n, slot in reversed(turns):
        out_ref[slot, 0] = total.astype(BF16)
        total = total + q_ref[n].astype(F32)
    done_ref[...] = jnp.zeros(done_ref.shape, F32)


def head_state(read, head, depth):
    parts = DH // depth
    if depth % HALO == 0:
        return jnp.concatenate([read(head * parts + n) for n in range(parts)], axis=0)
    found = [read(head * parts + n).astype(F32) for n in range(parts)]
    return jnp.concatenate(found, axis=0).astype(BF16)


def tap_kernel(
    core_ref,
    chip_ref,
    wide_ref,
    near_ref,
    edge_ref,
    out_ref,
    done_ref,
    taps_ref,
    *,
    scale,
    places,
    ways,
):
    depth = chip_ref.shape[2]
    size = out_ref.shape[1] - CW * HALF
    total = jnp.zeros((depth, DH), F32)
    for n, slot in places:
        out_ref[slot, :depth] = total.astype(BF16)
        if depth < size:
            out_ref[slot, depth:size] = jnp.zeros((size - depth, DH), BF16)
        total = total + chip_ref[n, 1].astype(F32)
    for i in range(HALF):
        suffix = head_state(lambda n: chip_ref[ways[n], 0], i, depth).astype(F32)
        add_taps(taps_ref, i, suffix, [wide_ref[i, j].astype(F32) for j in range(CW)])
    weights = (scale * (near_ref[...] + taps_ref[...])).astype(BF16)
    for n in range(out_ref.shape[0]):
        out_ref[n, size:] = weights
    done_ref[...] = jnp.zeros(done_ref.shape, F32)


def query_side_kernel(
    core_ref,
    chip_ref,
    k_ref,
    g_ref,
    head_ref,
    edge_ref,
    w_ref,
    done_ref,
    c_ref,
    gc_ref,
    q_ref,
    gk_ref,
    gv_ref,
    send_ref,
    gq_ref,
    own_ref,
    hold_ref,
    sems,
    fetch_sems,
    *,
    scale,
    ways,
):
    core = core_ref[0]
    rows = k_ref.shape[0]
    depth = chip_ref.shape[2]
    seen = later(rows)
    fetches = [
        pltpu.make_async_copy(ref, hold_ref.at[n], fetch_sems.at[n])
        for n, ref in enumerate((c_ref, q_ref, gc_ref))
    ]
    for fetch in fetches:
        fetch.start()
    for fetch in fetches:
        fetch.wait()
    for i in range(HALF):
        at = columns(i)
        suffix = head_state(lambda n: chip_ref[ways[n], 0], i, depth)
        c = jnp.concatenate([head_ref[:, at], hold_ref[0, HALO:, at]], axis=0)
        g, k = g_ref[:, at], k_ref[:, at]
        attn = jnp.where(seen.T, dot(g, c, (1, 1)), 0.0)
        gq_ref[:, at] = dot(attn.astype(BF16), k, (1, 0)).astype(BF16)
        turned = jnp.where(seen, dot(c, g, (1, 1)), 0.0)
        gk = dot(turned.astype(BF16), hold_ref[1, :, at], (1, 0))
        gk = scale * (gk + dot(c, suffix, (1, 1)))
        gc = scale * (hold_ref[2, :, at].astype(F32) + dot(k, suffix, (1, 0)))
        edge = edge_ref[...].astype(F32)[2 * EDGE * i : 2 * EDGE * (i + 1)]
        after = edge[:EDGE] + dot(edge.astype(BF16), suffix, (1, 0))[EDGE:]
        ext = jnp.concatenate([gc, scale * after, jnp.zeros((TILE - EDGE, DH), F32)], axis=0)
        taps = tap_rows(w_ref, core, i)
        gv = taps[0:1] * gc
        for j in range(1, CW):
            gv = gv + taps[j : j + 1] * ext[j : j + rows]
        for n, value in enumerate((gk, gv)):
            low, high = value[: rows // 2].astype(BF16), value[rows // 2 :].astype(BF16)
            own_ref[n, :, at] = jnp.where(core == 0, low, high)
            send_ref[n, :, at] = jnp.where(core == 0, high, low)
    put(own_ref, core, (gk_ref, gv_ref), sems)


def put(half_ref, side, refs, sems):
    copies = [
        pltpu.make_async_copy(half_ref.at[n], ref.at[:, half_of(side, WIDE)], sems.at[n])
        for n, ref in enumerate(refs)
    ]
    for copy in copies:
        copy.start()
    for copy in copies:
        copy.wait()


def key_side_kernel(
    core_ref, chip_ref, g_ref, gq_ref, own_ref, send_ref, taps_ref, *, scale, depth, slots
):
    core = core_ref[0]
    rows = g_ref.shape[0]
    chips, size, _ = chip_ref.shape
    for i in range(HALF):
        at = columns(i)
        prefix = head_state(lambda n: chip_ref[slots[n], :depth], i, depth)
        gq = scale * (gq_ref[:, at].astype(F32) + dot(g_ref[:, at], prefix, (1, 1)))
        low, high = gq[: rows // 2].astype(BF16), gq[rows // 2 :].astype(BF16)
        own_ref[:, at] = jnp.where(core == 0, low, high)
        send_ref[:, at] = jnp.where(core == 0, high, low)
    total = chip_ref[0, size - CW * HALF :].astype(F32)
    for n in range(1, chips):
        total = total + chip_ref[n, size - CW * HALF :].astype(F32)
    taps_ref[...] = total


def join_kernel(core_ref, recv_ref, own_ref, _, __, gk_ref, gv_ref, gq_ref, sems, sem):
    core = core_ref[0]
    copy = pltpu.make_async_copy(own_ref, gq_ref.at[:, half_of(core, WIDE)], sem)
    copy.start()
    put(recv_ref, 1 - core, (gk_ref, gv_ref), sems)
    copy.wait()


def finish_kernel(
    core_ref, recv_ref, taps_ref, far_ref, _, gq_ref, gw_ref, hold_ref, sems
):
    core = core_ref[0]
    place = gq_ref.at[:, half_of(1 - core, WIDE)]
    copies = [pltpu.make_async_copy(recv_ref, place, sems.at[0])]
    copies[0].start()
    for side, ref in ((core, taps_ref), (1 - core, far_ref)):
        for i in range(HALF):
            at = pl.ds(pl.multiple_of(side * WIDE + i * DH, DH), DH)
            for j in range(CW):
                row = j * HALF + i
                hold_ref[j : j + 1, at] = ref[row : row + 1, :]
    copies.append(pltpu.make_async_copy(hold_ref, gw_ref, sems.at[1]))
    copies[1].start()
    for copy in copies:
        copy.wait()


def local(queries, keys, values, grad_out, conv_weight):
    rows, width = queries.shape
    lines, line = lax.axis_size("row"), lax.axis_size("col") // 2
    count = 2 * lines * line
    chips = lines * line
    depth = WIDE // chips
    scale = (DH * rows * count) ** (-0.5)
    core = lax.rem(lax.axis_index("col"), 2).astype(jnp.int32).reshape(1)
    half = line // 2
    split = [*reversed(range(half)), *range(half, line)]
    spread = sorted(range(line), key=lambda z: (abs(2 * z + 1 - line), -z))
    mixed = [z for n in range(half) for z in (half + n, n)]
    lists = [
        [r * line + z for z in split for r in reversed(range(lines))],
        [r * line + z for r in reversed(range(lines)) for z in spread],
        [r * line + z for r in reversed(range(lines)) for z in mixed],
    ]
    groups = [[[2 * p + c for p in each] for c in range(2)] for each in lists]
    spots = [[each.index(p) for p in range(chips)] for each in lists]
    turns = tuple(zip(spots[0], spots[1]))
    places = tuple(zip(spots[1], spots[2]))
    ways = tuple(spots[1][p] for p in lists[0])
    slots = tuple(spots[2][p] for p in lists[1])

    def swap(value):
        return lax.ppermute(value, AXES, [(d, d ^ 1) for d in range(count)])

    def shifted(value, by):
        pairs = [(d, d + by) for d in range(count) if 0 <= d + by < count]
        return lax.ppermute(value, AXES, pairs)

    def turn(value, groups):
        return lax.all_to_all(value, AXES, 0, 0, axis_index_groups=groups, tiled=True)

    pair = shape((2, rows, WIDE))
    block = shape((2 * rows, WIDE))
    far_block = pltpu.HBM((2 * rows, WIDE), BF16)
    states = shape((HALF, DH, DH))
    edges = shape((HALO, WIDE))
    flag = shape((8, DH), F32)
    dma = pltpu.SemaphoreType.DMA
    padded = max(depth, HALO)

    def in_hbm(value):
        return pltpu.with_memory_space_constraint(value, pltpu.HBM)

    queries, grad_out, keys, values = map(in_hbm, (queries, grad_out, keys, values))
    q_keep, q_give = call(
        query_state_kernel,
        (states, states),
        core,
        [queries, grad_out],
        [pltpu.VMEM((2, rows, width), BF16), dma((2,))],
        [ANY] * 2,
    )
    q_recv = swap(q_give)
    longer = shape((2, rows + HALO, WIDE))
    kv_own, kv_send = call(
        split_key_kernel,
        (longer, longer),
        core,
        [keys, values, queries, grad_out, q_keep],
        [dma((2, 2, 2))],
        [ANY] * 4 + [VMEM],
    )
    kv_recv = swap(kv_send)
    q_sent, added = call(
        add_kernel,
        (states, flag),
        core,
        [q_keep, q_recv],
    )
    q_turned = turn(q_sent.reshape(chips, depth, DH), groups[0])
    tail = call(tail_kernel, shape((EDGE * HALF, DH)), core, [kv_own, kv_recv])
    k, v, edge = call(
        gather_key_kernel,
        (block, block, shape((2 * EDGE * HALF, DH))),
        core,
        [kv_own, kv_recv],
    )
    halo = shifted(tail, 2)
    c, k_state = call(
        conv_kernel,
        (far_block, shape((HALF, DH, DH), F32)),
        core,
        [k, v, conv_weight],
    )
    qg_own, qg_send = call(
        split_kernel,
        (pair, pair),
        core,
        [queries, grad_out, k_state],
        [dma((2, 2))],
        [ANY, ANY, VMEM],
    )
    qg_recv = swap(qg_send)
    q, g, q_far = call(
        gather_query_kernel,
        (block, block, far_block),
        core,
        [qg_own, qg_recv],
        [dma(())],
        made=(VMEM, VMEM, ANY),
    )
    both, c_head, turned = call(
        functools.partial(turn_kernel, turns=turns),
        (shape((chips, 2, depth, DH)), edges, flag),
        core,
        [q_turned, k_state, k, v, halo, conv_weight, qg_own],
    )
    both = turn(both, groups[1])
    gc, taps, wide = call(
        score_kernel,
        (far_block, shape((CW * HALF, DH), F32), shape((HALF, CW, DH, DH))),
        core,
        [q, g, k, v, halo]
    )
    edge = shifted(edge, -2)
    last, tapped = call(
        functools.partial(tap_kernel, scale=scale, places=places, ways=ways),
        (shape((chips, padded + CW * HALF, DH)), flag),
        core,
        [both, wide, taps, edge],
        [pltpu.VMEM((CW * HALF, DH), F32)],
    )
    last = turn(last, groups[2])
    full = shape((rows, width))
    grad_keys, grad_values, kv_give, gq = call(
        functools.partial(query_side_kernel, scale=scale, ways=ways),
        (full, full, pair, block),
        core,
        [both, k, g, c_head, edge, conv_weight, tapped, *map(in_hbm, (c, gc, q_far))],
        [pltpu.VMEM((2, rows, WIDE), BF16), pltpu.VMEM((3, 2 * rows, WIDE), BF16)]
        + [dma((2,)), dma((3,))],
        [VMEM] * 7 + [ANY] * 3,
        (ANY, ANY, VMEM, VMEM),
    )
    kv_got = swap(kv_give)
    q_grad, q_give, taps = call(
        functools.partial(key_side_kernel, scale=scale, depth=depth, slots=slots),
        (shape((rows, WIDE)), shape((rows, WIDE)), shape((CW * HALF, DH), F32)),
        core,
        [last, g, gq],
    )
    q_got = swap(q_give)
    far = swap(taps)
    grad_keys, grad_values, grad_queries = call(
        join_kernel,
        (full, full, full),
        core,
        [kv_got, q_grad, grad_keys, grad_values],
        [dma((2,)), dma(())],
        [VMEM, VMEM, ANY, ANY],
        (ANY, ANY, ANY),
        {3: 0, 4: 1},
    )
    grad_queries, grad_weight = call(
        finish_kernel,
        (full, shape((CW, width), F32)),
        core,
        [q_got, taps, far, grad_queries],
        [pltpu.VMEM((CW, width), F32), dma((2,))],
        [VMEM, VMEM, VMEM, ANY],
        (ANY, ANY),
        {4: 0},
    )
    return grad_queries, grad_keys, grad_values, grad_weight


def solution(mesh):
    placed = (
        P(("row", "col"), None),
        P(("row", "col"), None),
        P(("row", "col"), None),
        P(("row", "col"), None),
        P(),
    )
    return jax.shard_map(
        local,
        mesh=mesh,
        in_specs=placed,
        out_specs=(P(("row", "col"), None), P(("row", "col"), None), P(("row", "col"), None), P()),
        check_vma=False,
    )
```
